32 devices in a mesh: gx: 8 (over y, x, core), gz: 4 (over z).
Axes of the slice: x: 2, y: 2, z: 4, core: 2. Of those that a mesh axis runs over, the one named last changes fastest.
Arguments:
- density: float32 [512, 8, 1024], P('gx', None, 'gz'), may hold values from 0.5 to 2
- momentum: float32 [3, 512, 8, 1024], P(None, 'gx', None, 'gz'), may hold values from -5 to 5
- energy: float32 [512, 8, 1024], P('gx', None, 'gz'), may hold values from 2 to 6
- register: float32 [5, 512, 8, 1024], P(None, 'gx', None, 'gz'), may hold values from -6 to 6
Outputs:
- state: float32 [5, 512, 8, 1024], P(None, 'gx', None, 'gz')
- register_out: float32 [5, 512, 8, 1024], P(None, 'gx', None, 'gz')
The draws below stay inside these ranges and needn't reach their ends.
All inputs are finite; a program needn't handle non-finite values.
Results may differ from the reference program's by a relative error of at most 0.00005.
Values sent between devices are 32-bit elements; how exact they have to be, the bound alone decides.
A program may use at most 64 MiB of HBM per device.

```python
import jax
import jax.numpy as jnp
from jax import lax

YW = 8
NX = 512
NZ = 1024


def level_of(stream_key, shape, shards, smallest, high):
    def one(axis_at, shards_of):
        draws = jax.random.uniform(jax.random.fold_in(jax.random.fold_in(stream_key, 6), axis_at), (shards_of,), jnp.float32, smallest / len(shards), high / len(shards))
        return jnp.repeat(jnp.exp(draws), shape[axis_at] // shards_of).reshape((-1,) + (1,) * (len(shape) - axis_at - 1))

    loudness = one(*shards[0])
    for cut in shards[1:]:
        loudness = loudness * one(*cut)
    return loudness


def bell_draw(key, extent, deviation, bound, cuts=(), kind=jnp.bfloat16):
    drawn = jax.random.normal(key, extent, jnp.float32) * deviation
    if len(cuts) > 0:
        drawn = level_of(key, extent, cuts, -0.22, 0.18) * drawn
    return jnp.clip(drawn, min=-bound, max=bound).astype(kind)


def setup_inputs(seed: int = 0) -> dict:
    keys = jax.random.split(jax.random.key(seed), 5)
    density = jnp.clip(0.5 + 1.5 * jax.random.uniform(keys[0], (NX, YW, NZ), jnp.float32) ** level_of(keys[0], (NX, YW, NZ), ((0, 8), (2, 4)), -0.2, 0.2), 0.5, 2.0)
    momentum = bell_draw(keys[1], (3, NX, YW, NZ), 1.0, 5.0, ((1, 8), (3, 4)), jnp.float32)
    energy = jnp.clip(2.0 + 4.0 * jax.random.uniform(keys[2], (NX, YW, NZ), jnp.float32) ** level_of(keys[2], (NX, YW, NZ), ((0, 8), (2, 4)), -0.2, 0.2), 2.0, 6.0)
    register = bell_draw(keys[3], (5, NX, YW, NZ), 1.0, 6.0, ((1, 8), (3, 4)), jnp.float32)
    return {"density": density, "momentum": momentum, "energy": energy, "register": register}


lele_alpha = 0.45
coef_near = 49.0 / 60.0
coef_far = 1.0 / 15.0

def cyclic_solve(rhs):
    batch = rhs.shape[0]
    count = rhs.shape[1]
    index = jnp.arange(count)
    diag = jnp.where(index == 0, 2.0, jnp.where(index == count - 1, 1.0 + lele_alpha * lele_alpha, 1.0)).astype(rhs.dtype)
    lower = jnp.where(index == 0, 0.0, lele_alpha).astype(rhs.dtype)
    upper = jnp.where(index == count - 1, 0.0, lele_alpha).astype(rhs.dtype)
    diag_b = jnp.broadcast_to(diag, (batch, count))
    lower_b = jnp.broadcast_to(lower, (batch, count))
    upper_b = jnp.broadcast_to(upper, (batch, count))
    first = lax.linalg.tridiagonal_solve(lower_b, diag_b, upper_b, rhs)
    unit = jnp.where(index == 0, -1.0, jnp.where(index == count - 1, lele_alpha, 0.0)).astype(rhs.dtype)
    unit_b = jnp.broadcast_to(unit[None, :, None], (batch, count, 1))
    second = lax.linalg.tridiagonal_solve(lower_b, diag_b, upper_b, unit_b)
    factor = (first[:, 0:1, :] - lele_alpha * first[:, count - 1:count, :]) / (1.0 + second[:, 0:1, :] - lele_alpha * second[:, count - 1:count, :])
    return first - factor * second

def derivative(field):
    stencil = coef_near * (jnp.roll(field, -1, axis=1) - jnp.roll(field, 1, axis=1))
    stencil = stencil + coef_far * (jnp.roll(field, -2, axis=1) - jnp.roll(field, 2, axis=1))
    return cyclic_solve(stencil)

def plane(inputs):
    density, momentum, energy, register = inputs
    inverse_rho = 1.0 / density
    moment_x = momentum[0]
    moment_y = momentum[1]
    moment_z = momentum[2]
    pressure = 0.4 * (energy - 0.5 * (moment_x * moment_x + moment_y * moment_y + moment_z * moment_z) * inverse_rho)
    velocity_x = moment_x * inverse_rho
    velocity_z = moment_z * inverse_rho
    enthalpy = energy + pressure
    flux_x = jnp.stack([moment_x, moment_x * velocity_x + pressure, moment_y * velocity_x, moment_z * velocity_x, enthalpy * velocity_x])
    flux_z = jnp.stack([moment_z, moment_x * velocity_z, moment_y * velocity_z, moment_z * velocity_z + pressure, enthalpy * velocity_z])
    deriv_x = derivative(flux_x)
    deriv_z = jnp.swapaxes(derivative(jnp.swapaxes(flux_z, 1, 2)), 1, 2)
    rate = -(deriv_x + deriv_z)
    register_out = -(5.0 / 9.0) * register + 0.2 * rate
    fields = jnp.concatenate([density[None], momentum, energy[None]], axis=0)
    state = fields + 15.0 / 16.0 * register_out
    return (state, register_out)

def reference(density, momentum, energy, register):
    inputs = (jnp.transpose(density, (1, 0, 2)), jnp.transpose(momentum, (2, 0, 1, 3)), jnp.transpose(energy, (1, 0, 2)), jnp.transpose(register, (2, 0, 1, 3)))
    state, register_out = lax.map(plane, inputs)
    return (jnp.transpose(state, (1, 2, 0, 3)), jnp.transpose(register_out, (1, 2, 0, 3)))
```

```python
import functools

import jax
import jax.numpy as jnp
import numpy as np
from jax import lax
from jax.experimental import pallas as pl
from jax.experimental.pallas import tpu as pltpu
from jax.sharding import PartitionSpec as P

ALPHA = 0.45
NEAR = 49.0 / 60.0
FAR = 1.0 / 15.0
STEP = 0.2
CHUNK = 16

ROOT = (np.sqrt(1.0 - 4.0 * ALPHA * ALPHA) - 1.0) / (2.0 * ALPHA)
NORM = 1.0 / np.sqrt(1.0 - 4.0 * ALPHA * ALPHA)
GEOM = NORM * (NEAR * (1.0 / ROOT - ROOT) + FAR * (ROOT**-2 - ROOT**2))
EXTRA = NORM * FAR * (ROOT - 1.0 / ROOT)
SUM_COEF = -STEP * GEOM * ROOT
DIFF_COEF = -STEP * EXTRA


def split(values):
    high = np.asarray(values, np.float32).astype(jnp.bfloat16)
    low = (np.asarray(values, np.float64) - high.astype(np.float64)).astype(jnp.bfloat16)
    return high, low


def summary_table(count):
    cols = np.arange(count)
    rows = np.zeros((4, count))
    rows[0] = ROOT ** (count - 1 - cols)
    rows[1, count - 1] = 1.0
    rows[2] = ROOT**cols
    rows[3, 0] = 1.0
    high, low = split(rows)
    out = np.zeros((16, count), jnp.bfloat16)
    out[0:4] = high
    out[4:8] = low
    return out


def correction_table(count):
    cols = np.arange(count)
    rows = np.zeros((4, count))
    rows[0] = -SUM_COEF * ROOT**cols
    rows[1, 0] = -DIFF_COEF
    rows[2] = SUM_COEF * ROOT ** (count - 1 - cols)
    rows[3, count - 1] = DIFF_COEF
    high, low = split(rows)
    out = np.zeros((16, count), jnp.bfloat16)
    out[0:4] = high
    out[4:8] = high
    out[8:12] = low
    return out


def local_table(count):
    offset = np.arange(count)[:, None] - np.arange(count)[None, :]
    reach = np.abs(offset)
    values = SUM_COEF * np.power(ROOT, np.maximum(reach - 1, 0)) + DIFF_COEF * (reach == 1)
    return split(np.sign(offset) * values)


def weight_table(chunks):
    out = np.zeros((chunks, chunks + 3), np.float32)
    for c in range(chunks):
        for k in range(c + 1, chunks):
            out[c, k] = ROOT ** ((k - c - 1) * CHUNK)
        out[c, chunks] = ROOT ** ((chunks - 1 - c) * CHUNK)
        out[c, chunks + 1] = ROOT ** (c * CHUNK)
        out[c, chunks + 2] = 1.0 if c > 0 else 0.0
    return out


def fluxes(rho, mx, my, mz, energy):
    inverse = 1.0 / rho
    vx = mx * inverse
    vz = mz * inverse
    pressure = 0.4 * (energy - 0.5 * (mx * mx + my * my + mz * mz) * inverse)
    total = energy + pressure
    fx = (mx, mx * vx + pressure, my * vx, mz * vx, total * vx)
    fz = (mz, mx * vz, my * vz, mz * vz + pressure, total * vz)
    return fx, fz


def summary_kernel(w_ref, rho_ref, mom_ref, en_ref, zw_ref, b_ref, xr_ref, xl_ref, zr_ref, zl_ref):
    c = pl.program_id(0)
    fx, fz = fluxes(rho_ref[...], mom_ref[0], mom_ref[1], mom_ref[2], en_ref[...])
    carry_weight = w_ref[c, w_ref.shape[1] - 1]
    total_weight = w_ref[c, w_ref.shape[1] - 2]
    zw = zw_ref[...]
    rows = fz[0].shape[0] * fz[0].shape[1]
    for k in range(5):
        f = fx[k]
        left = jnp.where(carry_weight > 0.0, xr_ref[0, k], 0.0)
        for i in range(CHUNK):
            left = f[i] + ROOT * left
        right = f[CHUNK - 1]
        for i in range(CHUNK - 2, -1, -1):
            right = f[i] + ROOT * right
        b_ref[0, 0, k] = left
        b_ref[0, 1, k] = f[CHUNK - 1]
        b_ref[0, 2, k] = right
        b_ref[0, 3, k] = f[0]
        xr_ref[0, k] = left
        xr_ref[1, k] = f[CHUNK - 1]
        base = jnp.where(carry_weight > 0.0, xl_ref[0, k], 0.0)
        xl_ref[0, k] = base + total_weight * right
        xl_ref[1, k] = jnp.where(carry_weight > 0.0, xl_ref[1, k], f[0])

        g = fz[k].reshape(rows, fz[k].shape[2])
        high = g.astype(jnp.bfloat16)
        low = (g - high.astype(jnp.float32)).astype(jnp.bfloat16)
        dims = (((1,), (1,)), ((), ()))
        first = lax.dot_general(zw, high, dims, preferred_element_type=jnp.float32)
        second = lax.dot_general(zw, low, dims, preferred_element_type=jnp.float32)
        both = first[0:4] + first[4:8] + second[0:4]
        zr_ref[0, :, k * rows : (k + 1) * rows] = both[0:2]
        zl_ref[0, :, k * rows : (k + 1) * rows] = both[2:4]


def final_kernel(
    w_ref, rho_ref, mom_ref, en_ref, reg_ref, b_ref, xr_ref, xl_ref, zr_ref, zl_ref,
    hh_ref, hl_ref, cz_ref, state_ref, out_ref, stack_ref, left_ref,
):
    c = pl.program_id(0)
    chunks = b_ref.shape[0]
    fx, fz = fluxes(rho_ref[...], mom_ref[0], mom_ref[1], mom_ref[2], en_ref[...])
    fields = (rho_ref, mom_ref.at[0], mom_ref.at[1], mom_ref.at[2], en_ref)
    rows = fz[0].shape[0] * fz[0].shape[1]
    before = jnp.maximum(c - 1, 0)
    after = jnp.minimum(c + 1, chunks - 1)

    zr = zr_ref[0]
    zl = zl_ref[0]
    zr_high = zr.astype(jnp.bfloat16).astype(jnp.float32)
    zl_high = zl.astype(jnp.bfloat16).astype(jnp.float32)
    stack_ref[0:2] = zr_high
    stack_ref[2:4] = zl_high
    stack_ref[4:6] = zr - zr_high
    stack_ref[6:8] = zl - zl_high
    stack_ref[8:10] = zr_high
    stack_ref[10:12] = zl_high
    stack_ref[12:16] = jnp.zeros((4, stack_ref.shape[1]), jnp.float32)
    edges = stack_ref[...].astype(jnp.bfloat16)

    hh = hh_ref[...]
    hl = hl_ref[...]
    cz = cz_ref[...]
    for k in range(5):
        g = fz[k].reshape(rows, fz[k].shape[2])
        high = g.astype(jnp.bfloat16)
        low = (g - high.astype(jnp.float32)).astype(jnp.bfloat16)
        dz = jnp.dot(high, hh, preferred_element_type=jnp.float32)
        dz += jnp.dot(low, hh, preferred_element_type=jnp.float32)
        dz += jnp.dot(high, hl, preferred_element_type=jnp.float32)
        dz += lax.dot_general(
            edges[:, k * rows : (k + 1) * rows], cz, (((0,), (0,)), ((), ())),
            preferred_element_type=jnp.float32,
        )
        dz = dz.reshape(fz[k].shape)

        f = fx[k]
        left = w_ref[c, chunks + 1] * xr_ref[0, k] + w_ref[c, chunks + 2] * b_ref[before, 0, k]
        left_edge = jnp.where(c == 0, xr_ref[1, k], b_ref[before, 1, k])
        right = w_ref[c, chunks] * xl_ref[0, k]
        for m in range(1, chunks):
            right += w_ref[c, m] * b_ref[m, 2, k]
        right_edge = jnp.where(c == chunks - 1, xl_ref[1, k], b_ref[after, 3, k])
        for i in range(CHUNK):
            left_ref[i] = left
            left = f[i] + ROOT * left
        for i in range(CHUNK - 1, -1, -1):
            upper = f[i + 1] if i < CHUNK - 1 else right_edge
            lower = f[i - 1] if i > 0 else left_edge
            rate = SUM_COEF * (right - left_ref[i]) + DIFF_COEF * (upper - lower) + dz[i]
            fresh = rate - (5.0 / 9.0) * reg_ref[k, i]
            out_ref[k, i] = fresh
            state_ref[k, i] = fields[k][i] + (15.0 / 16.0) * fresh
            right = f[i] + ROOT * right


def shift(value, axis, step):
    count = lax.axis_size(axis)
    return lax.ppermute(value, axis, [(i, (i + step) % count) for i in range(count)])


def per_device(density, momentum, energy, register):
    nx, ny, nz = density.shape
    chunks = nx // CHUNK
    rows = CHUNK * ny
    f32 = jnp.float32
    plane = pl.BlockSpec((CHUNK, ny, nz), lambda c: (c, 0, 0))
    triple = pl.BlockSpec((3, CHUNK, ny, nz), lambda c: (0, c, 0, 0))
    quint = pl.BlockSpec((5, CHUNK, ny, nz), lambda c: (0, c, 0, 0))
    edge_x = pl.BlockSpec((2, 5, ny, nz), lambda c: (0, 0, 0, 0))
    edge_z = pl.BlockSpec((1, 2, 5 * rows), lambda c: (c, 0, 0))
    table = lambda shape: pl.BlockSpec(shape, lambda c: (0,) * len(shape))
    smem = pl.BlockSpec(memory_space=pltpu.SMEM)
    weights = jnp.asarray(weight_table(chunks))
    params = pltpu.CompilerParams(
        dimension_semantics=("arbitrary",), vmem_limit_bytes=40 * 1024 * 1024
    )

    bounds, xr, xl, zr, zl = pl.pallas_call(
        summary_kernel,
        grid=(chunks,),
        in_specs=[smem, plane, triple, plane, table((16, nz))],
        out_specs=[
            pl.BlockSpec((1, 4, 5, ny, nz), lambda c: (c, 0, 0, 0, 0)),
            edge_x, edge_x, edge_z, edge_z,
        ],
        out_shape=[
            jax.ShapeDtypeStruct((chunks, 4, 5, ny, nz), f32),
            jax.ShapeDtypeStruct((2, 5, ny, nz), f32),
            jax.ShapeDtypeStruct((2, 5, ny, nz), f32),
            jax.ShapeDtypeStruct((chunks, 2, 5 * rows), f32),
            jax.ShapeDtypeStruct((chunks, 2, 5 * rows), f32),
        ],
        compiler_params=params,
        name="summaries",
    )(weights, density, momentum, energy, jnp.asarray(summary_table(nz)))

    xr = shift(xr, "gx", 1)
    xl = shift(xl, "gx", -1)
    zr = shift(zr, "gz", 1)
    zl = shift(zl, "gz", -1)

    high, low = local_table(nz)
    return pl.pallas_call(
        final_kernel,
        grid=(chunks,),
        in_specs=[
            smem, plane, triple, plane, quint,
            table((chunks, 4, 5, ny, nz)), edge_x, edge_x, edge_z, edge_z,
            table((nz, nz)), table((nz, nz)), table((16, nz)),
        ],
        out_specs=[quint, quint],
        out_shape=[jax.ShapeDtypeStruct((5, nx, ny, nz), f32)] * 2,
        scratch_shapes=[
            pltpu.VMEM((16, 5 * rows), f32),
            pltpu.VMEM((CHUNK, ny, nz), f32),
        ],
        compiler_params=params,
        name="section",
    )(
        weights, density, momentum, energy, register, bounds, xr, xl, zr, zl,
        jnp.asarray(high), jnp.asarray(low), jnp.asarray(correction_table(nz)),
    )


def solution(mesh):
    specs = (
        P("gx", None, "gz"),
        P(None, "gx", None, "gz"),
        P("gx", None, "gz"),
        P(None, "gx", None, "gz"),
    )
    out = P(None, "gx", None, "gz")
    return jax.shard_map(
        per_device, mesh=mesh, in_specs=specs, out_specs=(out, out), check_vma=False
    )
```

```python
import functools

import jax
import jax.numpy as jnp
import numpy as np
from jax import lax
from jax.experimental import pallas as pl
from jax.experimental.pallas import tpu as pltpu
from jax.sharding import PartitionSpec as P

ALPHA = 0.45
NEAR = 49.0 / 60.0
FAR = 1.0 / 15.0
STEP = 0.2
CHUNK = 16

ROOT = (np.sqrt(1.0 - 4.0 * ALPHA * ALPHA) - 1.0) / (2.0 * ALPHA)
NORM = 1.0 / np.sqrt(1.0 - 4.0 * ALPHA * ALPHA)
GEOM = NORM * (NEAR * (1.0 / ROOT - ROOT) + FAR * (ROOT**-2 - ROOT**2))
EXTRA = NORM * FAR * (ROOT - 1.0 / ROOT)
SUM_COEF = -STEP * GEOM * ROOT
DIFF_COEF = -STEP * EXTRA


def split(values):
    high = np.asarray(values, np.float32).astype(jnp.bfloat16)
    low = (np.asarray(values, np.float64) - high.astype(np.float64)).astype(jnp.bfloat16)
    return high, low


def summary_table(count):
    cols = np.arange(count)
    rows = np.zeros((4, count))
    rows[0] = ROOT ** (count - 1 - cols)
    rows[1, count - 1] = 1.0
    rows[2] = ROOT**cols
    rows[3, 0] = 1.0
    high, low = split(rows)
    out = np.zeros((16, count), jnp.bfloat16)
    out[0:4] = high
    out[4:8] = low
    return out


def correction_table(count):
    cols = np.arange(count)
    rows = np.zeros((4, count))
    rows[0] = -SUM_COEF * ROOT**cols
    rows[1, 0] = -DIFF_COEF
    rows[2] = SUM_COEF * ROOT ** (count - 1 - cols)
    rows[3, count - 1] = DIFF_COEF
    high, low = split(rows)
    out = np.zeros((16, count), jnp.bfloat16)
    out[0:4] = high
    out[4:8] = high
    out[8:12] = low
    return out


def local_table(count):
    offset = np.arange(count)[:, None] - np.arange(count)[None, :]
    reach = np.abs(offset)
    values = SUM_COEF * np.power(ROOT, np.maximum(reach - 1, 0)) + DIFF_COEF * (reach == 1)
    return split(np.sign(offset) * values)


def weight_table(chunks):
    out = np.zeros((chunks, chunks + 3), np.float32)
    for c in range(chunks):
        for k in range(c + 1, chunks):
            out[c, k] = ROOT ** ((k - c - 1) * CHUNK)
        out[c, chunks] = ROOT ** ((chunks - 1 - c) * CHUNK)
        out[c, chunks + 1] = ROOT ** (c * CHUNK)
        out[c, chunks + 2] = 1.0 if c > 0 else 0.0
    return out


def fluxes(rho, mx, my, mz, energy):
    inverse = 1.0 / rho
    vx = mx * inverse
    vz = mz * inverse
    pressure = 0.4 * (energy - 0.5 * (mx * mx + my * my + mz * mz) * inverse)
    total = energy + pressure
    fx = (mx, mx * vx + pressure, my * vx, mz * vx, total * vx)
    fz = (mz, mx * vz, my * vz, mz * vz + pressure, total * vz)
    return fx, fz


def summary_kernel(
    w_ref, rho_ref, mom_ref, en_ref, zw_ref, b_ref, xr_out, xl_out, zr_out, zl_out,
    xr_ref, xl_ref, zr_ref, zl_ref, xr_got, xl_got, zr_got, zl_got, send_sem, recv_sem,
):
    c = pl.program_id(0)
    last = pl.num_programs(0) - 1
    gx, gz = lax.axis_index("gx"), lax.axis_index("gz")
    nx, nz = lax.axis_size("gx"), lax.axis_size("gz")
    x_next, x_prev = lax.rem(gx + 1, nx), lax.rem(gx + nx - 1, nx)
    z_next, z_prev = lax.rem(gz + 1, nz), lax.rem(gz + nz - 1, nz)
    neighbours = ((x_next, gz), (x_prev, gz), (gx, z_next), (gx, z_prev))
    barrier = pltpu.get_barrier_semaphore()

    @pl.when(c == 0)
    def _():
        for target in neighbours:
            pl.semaphore_signal(
                barrier, inc=1, device_id=target, device_id_type=pl.DeviceIdType.MESH
            )
        xr_ref[...] = jnp.zeros_like(xr_ref)
        xl_ref[...] = jnp.zeros_like(xl_ref)

    fx, fz = fluxes(rho_ref[...], mom_ref[0], mom_ref[1], mom_ref[2], en_ref[...])
    carry_weight = w_ref[c, w_ref.shape[1] - 1]
    total_weight = w_ref[c, w_ref.shape[1] - 2]
    zw = zw_ref[...]
    rows = fz[0].shape[0] * fz[0].shape[1]
    for k in range(5):
        f = fx[k]
        left = xr_ref[0, k]
        for i in range(CHUNK):
            left = f[i] + ROOT * left
        right = f[CHUNK - 1]
        for i in range(CHUNK - 2, -1, -1):
            right = f[i] + ROOT * right
        b_ref[0, 0, k] = left
        b_ref[0, 1, k] = f[CHUNK - 1]
        b_ref[0, 2, k] = right
        b_ref[0, 3, k] = f[0]
        xr_ref[0, k] = left
        xr_ref[1, k] = f[CHUNK - 1]
        xl_ref[0, k] = xl_ref[0, k] + total_weight * right
        xl_ref[1, k] = xl_ref[1, k] + (1.0 - carry_weight) * f[0]

        g = fz[k].reshape(rows, fz[k].shape[2])
        high = g.astype(jnp.bfloat16)
        low = (g - high.astype(jnp.float32)).astype(jnp.bfloat16)
        dims = (((1,), (1,)), ((), ()))
        first = lax.dot_general(zw, high, dims, preferred_element_type=jnp.float32)
        second = lax.dot_general(zw, low, dims, preferred_element_type=jnp.float32)
        both = first[0:4] + first[4:8] + second[0:4]
        zr_ref[c, :, k * rows : (k + 1) * rows] = both[0:2]
        zl_ref[c, :, k * rows : (k + 1) * rows] = both[2:4]

    @pl.when(c == last)
    def _():
        pl.semaphore_wait(barrier, 4)
        copies = []
        pairs = ((xr_ref, xr_got), (xl_ref, xl_got), (zr_ref, zr_got), (zl_ref, zl_got))
        for n, (source, target) in enumerate(pairs):
            copy = pltpu.make_async_remote_copy(
                src_ref=source,
                dst_ref=target,
                send_sem=send_sem.at[n],
                recv_sem=recv_sem.at[n],
                device_id=neighbours[n],
                device_id_type=pl.DeviceIdType.MESH,
            )
            copy.start()
            copies.append(copy)
        for copy in copies:
            copy.wait()
        xr_out[...] = xr_got[...]
        xl_out[...] = xl_got[...]
        zr_out[...] = zr_got[...]
        zl_out[...] = zl_got[...]


def final_kernel(
    w_ref, rho_ref, mom_ref, en_ref, reg_ref, b_ref, xr_ref, xl_ref, zr_ref, zl_ref,
    hh_ref, hl_ref, cz_ref, state_ref, out_ref, stack_ref, left_ref,
):
    c = pl.program_id(0)
    chunks = b_ref.shape[0]
    fx, fz = fluxes(rho_ref[...], mom_ref[0], mom_ref[1], mom_ref[2], en_ref[...])
    fields = (rho_ref, mom_ref.at[0], mom_ref.at[1], mom_ref.at[2], en_ref)
    rows = fz[0].shape[0] * fz[0].shape[1]
    before = jnp.maximum(c - 1, 0)
    after = jnp.minimum(c + 1, chunks - 1)

    zr = zr_ref[0]
    zl = zl_ref[0]
    zr_high = zr.astype(jnp.bfloat16).astype(jnp.float32)
    zl_high = zl.astype(jnp.bfloat16).astype(jnp.float32)
    stack_ref[0:2] = zr_high
    stack_ref[2:4] = zl_high
    stack_ref[4:6] = zr - zr_high
    stack_ref[6:8] = zl - zl_high
    stack_ref[8:10] = zr_high
    stack_ref[10:12] = zl_high
    stack_ref[12:16] = jnp.zeros((4, stack_ref.shape[1]), jnp.float32)
    edges = stack_ref[...].astype(jnp.bfloat16)

    hh = hh_ref[...]
    hl = hl_ref[...]
    cz = cz_ref[...]
    for k in range(5):
        g = fz[k].reshape(rows, fz[k].shape[2])
        high = g.astype(jnp.bfloat16)
        low = (g - high.astype(jnp.float32)).astype(jnp.bfloat16)
        dz = jnp.dot(high, hh, preferred_element_type=jnp.float32)
        dz += jnp.dot(low, hh, preferred_element_type=jnp.float32)
        dz += jnp.dot(high, hl, preferred_element_type=jnp.float32)
        dz += lax.dot_general(
            edges[:, k * rows : (k + 1) * rows], cz, (((0,), (0,)), ((), ())),
            preferred_element_type=jnp.float32,
        )
        dz = dz.reshape(fz[k].shape)

        f = fx[k]
        left = w_ref[c, chunks + 1] * xr_ref[0, k] + w_ref[c, chunks + 2] * b_ref[before, 0, k]
        left_edge = jnp.where(c == 0, xr_ref[1, k], b_ref[before, 1, k])
        right = w_ref[c, chunks] * xl_ref[0, k]
        for m in range(1, chunks):
            right += w_ref[c, m] * b_ref[m, 2, k]
        right_edge = jnp.where(c == chunks - 1, xl_ref[1, k], b_ref[after, 3, k])
        for i in range(CHUNK):
            left_ref[i] = left
            left = f[i] + ROOT * left
        for i in range(CHUNK - 1, -1, -1):
            upper = f[i + 1] if i < CHUNK - 1 else right_edge
            lower = f[i - 1] if i > 0 else left_edge
            rate = SUM_COEF * (right - left_ref[i]) + DIFF_COEF * (upper - lower) + dz[i]
            fresh = rate - (5.0 / 9.0) * reg_ref[k, i]
            out_ref[k, i] = fresh
            state_ref[k, i] = fields[k][i] + (15.0 / 16.0) * fresh
            right = f[i] + ROOT * right


def per_device(density, momentum, energy, register):
    nx, ny, nz = density.shape
    chunks = nx // CHUNK
    rows = CHUNK * ny
    f32 = jnp.float32
    plane = pl.BlockSpec((CHUNK, ny, nz), lambda c: (c, 0, 0))
    triple = pl.BlockSpec((3, CHUNK, ny, nz), lambda c: (0, c, 0, 0))
    quint = pl.BlockSpec((5, CHUNK, ny, nz), lambda c: (0, c, 0, 0))
    edge_x = pl.BlockSpec((2, 5, ny, nz), lambda c: (0, 0, 0, 0))
    edge_z = pl.BlockSpec((1, 2, 5 * rows), lambda c: (c, 0, 0))
    table = lambda shape: pl.BlockSpec(shape, lambda c: (0,) * len(shape))
    smem = pl.BlockSpec(memory_space=pltpu.SMEM)
    weights = jnp.asarray(weight_table(chunks))
    params = functools.partial(
        pltpu.CompilerParams,
        dimension_semantics=("arbitrary",),
        vmem_limit_bytes=60 * 1024 * 1024,
    )
    whole_z = pl.BlockSpec((chunks, 2, 5 * rows), lambda c: (0, 0, 0))
    x_buffer = pltpu.VMEM((2, 5, ny, nz), f32)
    z_buffer = pltpu.VMEM((chunks, 2, 5 * rows), f32)

    bounds, xr, xl, zr, zl = pl.pallas_call(
        summary_kernel,
        grid=(chunks,),
        in_specs=[smem, plane, triple, plane, table((16, nz))],
        out_specs=[
            pl.BlockSpec((1, 4, 5, ny, nz), lambda c: (c, 0, 0, 0, 0)),
            edge_x, edge_x, whole_z, whole_z,
        ],
        out_shape=[
            jax.ShapeDtypeStruct((chunks, 4, 5, ny, nz), f32),
            jax.ShapeDtypeStruct((2, 5, ny, nz), f32),
            jax.ShapeDtypeStruct((2, 5, ny, nz), f32),
            jax.ShapeDtypeStruct((chunks, 2, 5 * rows), f32),
            jax.ShapeDtypeStruct((chunks, 2, 5 * rows), f32),
        ],
        scratch_shapes=[x_buffer, x_buffer, z_buffer, z_buffer] * 2
        + [pltpu.SemaphoreType.DMA((4,)), pltpu.SemaphoreType.DMA((4,))],
        compiler_params=params(collective_id=0, has_side_effects=True),
        name="summaries",
    )(weights, density, momentum, energy, jnp.asarray(summary_table(nz)))

    high, low = local_table(nz)
    return pl.pallas_call(
        final_kernel,
        grid=(chunks,),
        in_specs=[
            smem, plane, triple, plane, quint,
            table((chunks, 4, 5, ny, nz)), edge_x, edge_x, edge_z, edge_z,
            table((nz, nz)), table((nz, nz)), table((16, nz)),
        ],
        out_specs=[quint, quint],
        out_shape=[jax.ShapeDtypeStruct((5, nx, ny, nz), f32)] * 2,
        scratch_shapes=[
            pltpu.VMEM((16, 5 * rows), f32),
            pltpu.VMEM((CHUNK, ny, nz), f32),
        ],
        compiler_params=params(),
        name="section",
    )(
        weights, density, momentum, energy, register, bounds, xr, xl, zr, zl,
        jnp.asarray(high), jnp.asarray(low), jnp.asarray(correction_table(nz)),
    )


def solution(mesh):
    specs = (
        P("gx", None, "gz"),
        P(None, "gx", None, "gz"),
        P("gx", None, "gz"),
        P(None, "gx", None, "gz"),
    )
    out = P(None, "gx", None, "gz")
    return jax.shard_map(
        per_device, mesh=mesh, in_specs=specs, out_specs=(out, out), check_vma=False
    )
```

```python
import functools

import jax
import jax.numpy as jnp
import numpy as np
from jax import lax
from jax.experimental import pallas as pl
from jax.experimental.pallas import tpu as pltpu
from jax.sharding import PartitionSpec as P

ALPHA = 0.45
NEAR = 49.0 / 60.0
FAR = 1.0 / 15.0
STEP = 0.2
CHUNK = 16

ROOT = (np.sqrt(1.0 - 4.0 * ALPHA * ALPHA) - 1.0) / (2.0 * ALPHA)
NORM = 1.0 / np.sqrt(1.0 - 4.0 * ALPHA * ALPHA)
GEOM = NORM * (NEAR * (1.0 / ROOT - ROOT) + FAR * (ROOT**-2 - ROOT**2))
EXTRA = NORM * FAR * (ROOT - 1.0 / ROOT)
SUM_COEF = -STEP * GEOM * ROOT
DIFF_COEF = -STEP * EXTRA


def split(values):
    high = np.asarray(values, np.float32).astype(jnp.bfloat16)
    low = (np.asarray(values, np.float64) - high.astype(np.float64)).astype(jnp.bfloat16)
    return high, low


def summary_table(count):
    cols = np.arange(count)
    rows = np.zeros((4, count))
    rows[0] = ROOT ** (count - 1 - cols)
    rows[1, count - 1] = 1.0
    rows[2] = ROOT**cols
    rows[3, 0] = 1.0
    high, low = split(rows)
    out = np.zeros((16, count), jnp.bfloat16)
    out[0:4] = high
    out[4:8] = low
    return out


def correction_table(count):
    cols = np.arange(count)
    rows = np.zeros((4, count))
    rows[0] = -SUM_COEF * ROOT**cols
    rows[1, 0] = -DIFF_COEF
    rows[2] = SUM_COEF * ROOT ** (count - 1 - cols)
    rows[3, count - 1] = DIFF_COEF
    high, low = split(rows)
    out = np.zeros((16, count), jnp.bfloat16)
    out[0:4] = high
    out[4:8] = high
    out[8:12] = low
    return out


def local_table(count):
    offset = np.arange(count)[:, None] - np.arange(count)[None, :]
    reach = np.abs(offset)
    values = SUM_COEF * np.power(ROOT, np.maximum(reach - 1, 0)) + DIFF_COEF * (reach == 1)
    return split(np.sign(offset) * values)


def weight_table(chunks):
    out = np.zeros((chunks, 4), np.float32)
    for c in range(chunks):
        out[c, 0] = ROOT ** (c * CHUNK)
        out[c, 1] = ROOT ** ((chunks - 1 - c) * CHUNK)
        out[c, 2] = 1.0 if c == 0 else 0.0
        out[c, 3] = 1.0 if c == chunks - 1 else 0.0
    return out


def fluxes(rho, mx, my, mz, energy):
    inverse = 1.0 / rho
    vx = mx * inverse
    vz = mz * inverse
    pressure = 0.4 * (energy - 0.5 * (mx * mx + my * my + mz * mz) * inverse)
    total = energy + pressure
    fx = (mx, mx * vx + pressure, my * vx, mz * vx, total * vx)
    fz = (mz, mx * vz, my * vz, mz * vz + pressure, total * vz)
    return fx, fz


def local_kernel(
    w_ref, rho_ref, mom_ref, en_ref, reg_ref, zw_ref, hh_ref, hl_ref,
    part_ref, xr_out, xl_out, zr_out, zl_out,
    xr_ref, xl_ref, zr_ref, zl_ref, xr_got, xl_got, zr_got, zl_got,
    fx_ref, left_ref, high_ref, low_ref, dz_ref, carry_ref, send_sem, recv_sem,
):
    step = pl.program_id(0)
    chunks = high_ref.shape[0]
    cells, width, lanes = fx_ref.shape[0] - 2, fx_ref.shape[2], fx_ref.shape[3]
    rows = CHUNK * width
    gx, gz = lax.axis_index("gx"), lax.axis_index("gz")
    nx, nz = lax.axis_size("gx"), lax.axis_size("gz")
    x_next, x_prev = lax.rem(gx + 1, nx), lax.rem(gx + nx - 1, nx)
    z_next, z_prev = lax.rem(gz + 1, nz), lax.rem(gz + nz - 1, nz)
    neighbours = ((x_next, gz), (x_prev, gz), (gx, z_next), (gx, z_prev))
    barrier = pltpu.get_barrier_semaphore()
    pairs = ((xr_ref, xr_got), (xl_ref, xl_got), (zr_ref, zr_got), (zl_ref, zl_got))

    @pl.when(step == 0)
    def _():
        for target in neighbours:
            pl.semaphore_signal(
                barrier, inc=1, device_id=target, device_id_type=pl.DeviceIdType.MESH
            )
        xr_ref[...] = jnp.zeros_like(xr_ref)
        xl_ref[...] = jnp.zeros_like(xl_ref)
        carry_ref[...] = jnp.zeros_like(carry_ref)
        fx_ref[0] = jnp.zeros((5, width, lanes), jnp.float32)
        fx_ref[cells + 1] = jnp.zeros((5, width, lanes), jnp.float32)

    @pl.when(step < chunks)
    def _():
        start = step * CHUNK
        left = [xr_ref[0, k] for k in range(5)]
        right = [None] * 5
        first = [None] * 5
        for i in range(0, CHUNK, 2):
            fx, fz = fluxes(
                rho_ref[i : i + 2], mom_ref[0, i : i + 2], mom_ref[1, i : i + 2],
                mom_ref[2, i : i + 2], en_ref[i : i + 2],
            )
            for k in range(5):
                even, odd = fx[k][0], fx[k][1]
                fx_ref[start + i + 1, k] = even
                fx_ref[start + i + 2, k] = odd
                left_ref[start + i, k] = left[k]
                left[k] = even + ROOT * left[k]
                left_ref[start + i + 1, k] = left[k]
                left[k] = odd + ROOT * left[k]
                both = ROOT**i * even + ROOT ** (i + 1) * odd
                right[k] = both if i == 0 else right[k] + both
                if i == 0:
                    first[k] = even
                if i == CHUNK - 2:
                    xr_ref[1, k] = odd
                g = fz[k].reshape(2 * width, lanes)
                high = g.astype(jnp.bfloat16)
                low = (g - high.astype(jnp.float32)).astype(jnp.bfloat16)
                at = k * rows + i * width
                high_ref[step, at : at + 2 * width] = high
                low_ref[step, at : at + 2 * width] = low
        for k in range(5):
            xr_ref[0, k] = left[k]
            xl_ref[0, k] = xl_ref[0, k] + w_ref[step, 0] * right[k]
            xl_ref[1, k] = xl_ref[1, k] + w_ref[step, 2] * first[k]
        dims = (((1,), (1,)), ((), ()))
        zw = zw_ref[...]
        one = lax.dot_general(zw, high_ref[step], dims, preferred_element_type=jnp.float32)
        two = lax.dot_general(zw, low_ref[step], dims, preferred_element_type=jnp.float32)
        total = one[0:4] + one[4:8] + two[0:4]
        zr_ref[step] = total[0:2]
        zl_ref[step] = total[2:4]

    def copy_of(n):
        return pltpu.make_async_remote_copy(
            src_ref=pairs[n][0],
            dst_ref=pairs[n][1],
            send_sem=send_sem.at[n],
            recv_sem=recv_sem.at[n],
            device_id=neighbours[n],
            device_id_type=pl.DeviceIdType.MESH,
        )

    @pl.when(step == chunks - 1)
    def _():
        pl.semaphore_wait(barrier, 4)
        for n in range(4):
            copy_of(n).start()

    @pl.when(step >= chunks)
    def _():
        chunk = 2 * chunks - 1 - step
        start = chunk * CHUNK
        high = high_ref[chunk]
        hh = hh_ref[...]
        dz = jnp.dot(high, hh, preferred_element_type=jnp.float32)
        dz += jnp.dot(low_ref[chunk], hh, preferred_element_type=jnp.float32)
        dz += jnp.dot(high, hl_ref[...], preferred_element_type=jnp.float32)
        dz_ref[...] = dz.reshape(dz_ref.shape)
        right = carry_ref[...]
        upper = fx_ref[start + CHUNK + 1]
        here = fx_ref[start + CHUNK]
        for i in range(CHUNK - 1, -1, -1):
            lower = fx_ref[start + i]
            rate = SUM_COEF * (right - left_ref[start + i]) + DIFF_COEF * (upper - lower)
            part_ref[:, i] = rate + dz_ref[:, i] - (5.0 / 9.0) * reg_ref[:, i]
            right = here + ROOT * right
            upper = here
            here = lower
        carry_ref[...] = right

    @pl.when(step == 2 * chunks - 1)
    def _():
        for n in range(4):
            copy_of(n).wait()
        xr_out[...] = xr_got[...]
        xl_out[...] = xl_got[...]
        zr_out[...] = zr_got[...]
        zl_out[...] = zl_got[...]


def final_kernel(
    w_ref, rho_ref, mom_ref, en_ref, part_ref, xr_ref, xl_ref, zr_ref, zl_ref, cz_ref,
    state_ref, out_ref, stack_ref, dz_ref,
):
    c = pl.program_id(0)
    zr = zr_ref[0]
    zl = zl_ref[0]
    zr_high = zr.astype(jnp.bfloat16).astype(jnp.float32)
    zl_high = zl.astype(jnp.bfloat16).astype(jnp.float32)
    stack_ref[0:2] = zr_high
    stack_ref[2:4] = zl_high
    stack_ref[4:6] = zr - zr_high
    stack_ref[6:8] = zl - zl_high
    stack_ref[8:10] = zr_high
    stack_ref[10:12] = zl_high
    stack_ref[12:16] = jnp.zeros((4, stack_ref.shape[1]), jnp.float32)
    dz = lax.dot_general(
        stack_ref[...].astype(jnp.bfloat16), cz_ref[...], (((0,), (0,)), ((), ())),
        preferred_element_type=jnp.float32,
    )
    dz_ref[...] = dz.reshape(dz_ref.shape)
    left = (-SUM_COEF * w_ref[c, 0]) * xr_ref[0]
    right = (SUM_COEF * w_ref[c, 1]) * xl_ref[0]
    for i in range(CHUNK):
        fresh = part_ref[:, i] + dz_ref[:, i]
        fresh += ROOT**i * left + ROOT ** (CHUNK - 1 - i) * right
        if i == 0:
            fresh -= (DIFF_COEF * w_ref[c, 2]) * xr_ref[1]
        if i == CHUNK - 1:
            fresh += (DIFF_COEF * w_ref[c, 3]) * xl_ref[1]
        out_ref[:, i] = fresh
        scaled = (15.0 / 16.0) * fresh
        state_ref[0, i] = rho_ref[i] + scaled[0]
        for k in range(3):
            state_ref[k + 1, i] = mom_ref[k, i] + scaled[k + 1]
        state_ref[4, i] = en_ref[i] + scaled[4]


def per_device(density, momentum, energy, register):
    nx, ny, nz = density.shape
    chunks = nx // CHUNK
    rows = CHUNK * ny
    f32, bf16 = jnp.float32, jnp.bfloat16
    table = lambda shape: pl.BlockSpec(shape, lambda c: (0,) * len(shape))
    smem = pl.BlockSpec(memory_space=pltpu.SMEM)
    weights = jnp.asarray(weight_table(chunks))
    params = functools.partial(
        pltpu.CompilerParams,
        dimension_semantics=("arbitrary",),
        vmem_limit_bytes=60 * 1024 * 1024,
    )
    edge_x = (2, 5, ny, nz)
    edge_z = (chunks, 2, 5 * rows)
    buffers = [pltpu.VMEM(edge_x, f32)] * 2 + [pltpu.VMEM(edge_z, f32)] * 2
    high, low = local_table(nz)

    ahead = lambda s: jnp.minimum(s, chunks - 1)
    back = lambda s: jnp.minimum(2 * chunks - 1 - s, chunks - 1)
    quint = pl.BlockSpec((5, CHUNK, ny, nz), lambda s: (0, back(s), 0, 0))
    part, xr, xl, zr, zl = pl.pallas_call(
        local_kernel,
        grid=(2 * chunks,),
        in_specs=[
            smem,
            pl.BlockSpec((CHUNK, ny, nz), lambda s: (ahead(s), 0, 0)),
            pl.BlockSpec((3, CHUNK, ny, nz), lambda s: (0, ahead(s), 0, 0)),
            pl.BlockSpec((CHUNK, ny, nz), lambda s: (ahead(s), 0, 0)),
            quint, table((16, nz)), table((nz, nz)), table((nz, nz)),
        ],
        out_specs=[quint, table(edge_x), table(edge_x), table(edge_z), table(edge_z)],
        out_shape=[
            jax.ShapeDtypeStruct(shape, f32)
            for shape in ((5, nx, ny, nz), edge_x, edge_x, edge_z, edge_z)
        ],
        scratch_shapes=buffers * 2
        + [
            pltpu.VMEM((nx + 2, 5, ny, nz), f32),
            pltpu.VMEM((nx, 5, ny, nz), f32),
            pltpu.VMEM((chunks, 5 * rows, nz), bf16),
            pltpu.VMEM((chunks, 5 * rows, nz), bf16),
            pltpu.VMEM((5, CHUNK, ny, nz), f32),
            pltpu.VMEM((5, ny, nz), f32),
            pltpu.SemaphoreType.DMA((4,)),
            pltpu.SemaphoreType.DMA((4,)),
        ],
        compiler_params=params(collective_id=0, has_side_effects=True),
        name="local_part",
    )(
        weights, density, momentum, energy, register,
        jnp.asarray(summary_table(nz)), jnp.asarray(high), jnp.asarray(low),
    )

    plane = pl.BlockSpec((CHUNK, ny, nz), lambda c: (c, 0, 0))
    triple = pl.BlockSpec((3, CHUNK, ny, nz), lambda c: (0, c, 0, 0))
    quint = pl.BlockSpec((5, CHUNK, ny, nz), lambda c: (0, c, 0, 0))
    line_z = pl.BlockSpec((1, 2, 5 * rows), lambda c: (c, 0, 0))
    return pl.pallas_call(
        final_kernel,
        grid=(chunks,),
        in_specs=[
            smem, plane, triple, plane, quint, table(edge_x), table(edge_x),
            line_z, line_z, table((16, nz)),
        ],
        out_specs=[quint, quint],
        out_shape=[jax.ShapeDtypeStruct((5, nx, ny, nz), f32)] * 2,
        scratch_shapes=[
            pltpu.VMEM((16, 5 * rows), f32),
            pltpu.VMEM((5, CHUNK, ny, nz), f32),
        ],
        compiler_params=params(),
        name="neighbour_part",
    )(
        weights, density, momentum, energy, part, xr, xl, zr, zl,
        jnp.asarray(correction_table(nz)),
    )


def solution(mesh):
    specs = (
        P("gx", None, "gz"),
        P(None, "gx", None, "gz"),
        P("gx", None, "gz"),
        P(None, "gx", None, "gz"),
    )
    out = P(None, "gx", None, "gz")
    return jax.shard_map(
        per_device, mesh=mesh, in_specs=specs, out_specs=(out, out), check_vma=False
    )
```

```python
import jax
import jax.numpy as jnp
import numpy as np
from jax import lax
from jax.experimental import pallas as pl
from jax.experimental.pallas import tpu as pltpu
from jax.sharding import PartitionSpec as P

ALPHA = 0.45
NEAR = 49.0 / 60.0
FAR = 1.0 / 15.0
STEP = 0.2
CHUNK = 16

ROOT = (np.sqrt(1.0 - 4.0 * ALPHA * ALPHA) - 1.0) / (2.0 * ALPHA)
NORM = 1.0 / np.sqrt(1.0 - 4.0 * ALPHA * ALPHA)
GEOM = NORM * (NEAR * (1.0 / ROOT - ROOT) + FAR * (ROOT**-2 - ROOT**2))
EXTRA = NORM * FAR * (ROOT - 1.0 / ROOT)
SUM_COEF = -STEP * GEOM * ROOT
DIFF_COEF = -STEP * EXTRA


def split(values):
    high = np.asarray(values, np.float32).astype(jnp.bfloat16)
    low = (np.asarray(values, np.float64) - high.astype(np.float64)).astype(jnp.bfloat16)
    return high, low


def summary_table(count):
    cols = np.arange(count)
    rows = np.zeros((4, count))
    rows[0] = ROOT ** (count - 1 - cols)
    rows[1, count - 1] = 1.0
    rows[2] = ROOT**cols
    rows[3, 0] = 1.0
    high, low = split(rows)
    out = np.zeros((16, count), jnp.bfloat16)
    out[0:4] = high
    out[4:8] = low
    return out


def correction_table(count):
    cols = np.arange(count)
    rows = np.zeros((4, count))
    rows[0] = -SUM_COEF * ROOT**cols
    rows[1, 0] = -DIFF_COEF
    rows[2] = SUM_COEF * ROOT ** (count - 1 - cols)
    rows[3, count - 1] = DIFF_COEF
    high, low = split(rows)
    out = np.zeros((16, count), jnp.bfloat16)
    out[0:4] = high
    out[4:8] = high
    out[8:12] = low
    return out


def local_table(count):
    offset = np.arange(count)[:, None] - np.arange(count)[None, :]
    reach = np.abs(offset)
    values = SUM_COEF * np.power(ROOT, np.maximum(reach - 1, 0)) + DIFF_COEF * (reach == 1)
    return split(np.sign(offset) * values)


def weight_table(chunks):
    out = np.zeros((chunks, 4), np.float32)
    for c in range(chunks):
        out[c, 0] = ROOT ** (c * CHUNK)
        out[c, 1] = ROOT ** ((chunks - 1 - c) * CHUNK)
        out[c, 2] = 1.0 if c == 0 else 0.0
        out[c, 3] = 1.0 if c == chunks - 1 else 0.0
    return out


def fluxes(rho, mx, my, mz, energy):
    inverse = 1.0 / rho
    vx = mx * inverse
    vz = mz * inverse
    pressure = 0.4 * (energy - 0.5 * (mx * mx + my * my + mz * mz) * inverse)
    total = energy + pressure
    fx = (mx, mx * vx + pressure, my * vx, mz * vx, total * vx)
    fz = (mz, mx * vz, my * vz, mz * vz + pressure, total * vz)
    return fx, fz


def local_kernel(
    w_ref, rho_ref, mom_ref, en_ref, reg_ref, zw_ref, hh_ref, hl_ref,
    part_ref, xr_out, xl_out, zr_out, zl_out,
    xr_ref, xl_ref, zr_ref, zl_ref, xr_got, xl_got, zr_got, zl_got,
    fx_ref, left_ref, high_ref, low_ref, dz_ref, carry_ref,
    cell_ref, reg_buf, hh_buf, hl_buf, send_sem, recv_sem, load_sem, table_sem,
):
    step = pl.program_id(0)
    chunks = high_ref.shape[0]
    cells, width, lanes = fx_ref.shape[0] - 2, fx_ref.shape[2], fx_ref.shape[3]
    rows = CHUNK * width
    gx, gz = lax.axis_index("gx"), lax.axis_index("gz")
    nx, nz = lax.axis_size("gx"), lax.axis_size("gz")
    x_next, x_prev = lax.rem(gx + 1, nx), lax.rem(gx + nx - 1, nx)
    z_next, z_prev = lax.rem(gz + 1, nz), lax.rem(gz + nz - 1, nz)
    neighbours = ((x_next, gz), (x_prev, gz), (gx, z_next), (gx, z_prev))
    barrier = pltpu.get_barrier_semaphore()
    pairs = ((xr_ref, xr_got), (xl_ref, xl_got), (zr_ref, zr_got), (zl_ref, zl_got))

    def loads_of(chunk, first, stop):
        at = pl.ds(chunk * CHUNK, CHUNK)
        ends = (
            (rho_ref.at[at], cell_ref.at[0, at]),
            (mom_ref.at[:, at], cell_ref.at[1:4, at]),
            (en_ref.at[at], cell_ref.at[4, at]),
            (reg_ref.at[:, at], reg_buf.at[:, at]),
        )
        return [
            pltpu.make_async_copy(source, target, load_sem.at[chunk, n])
            for n, (source, target) in enumerate(ends)
            if first <= n < stop
        ]

    def table_loads():
        return (
            pltpu.make_async_copy(hh_ref, hh_buf, table_sem.at[0]),
            pltpu.make_async_copy(hl_ref, hl_buf, table_sem.at[1]),
        )

    @pl.when(step == 0)
    def _():
        for chunk in range(chunks):
            for copy in loads_of(chunk, 0, 3):
                copy.start()
        for copy in table_loads():
            copy.start()
        for chunk in range(chunks - 1, -1, -1):
            loads_of(chunk, 3, 4)[0].start()
        for target in neighbours:
            pl.semaphore_signal(
                barrier, inc=1, device_id=target, device_id_type=pl.DeviceIdType.MESH
            )
        xr_ref[...] = jnp.zeros_like(xr_ref)
        xl_ref[...] = jnp.zeros_like(xl_ref)
        carry_ref[...] = jnp.zeros_like(carry_ref)
        fx_ref[0] = jnp.zeros((5, width, lanes), jnp.float32)
        fx_ref[cells + 1] = jnp.zeros((5, width, lanes), jnp.float32)

    @pl.when(step < chunks)
    def _():
        start = step * CHUNK
        for copy in loads_of(step, 0, 3):
            copy.wait()
        left = [xr_ref[0, k] for k in range(5)]
        right = [None] * 5
        first = [None] * 5
        for i in range(0, CHUNK, 2):
            fx, fz = fluxes(*(cell_ref[k, pl.ds(start + i, 2)] for k in range(5)))
            for k in range(5):
                even, odd = fx[k][0], fx[k][1]
                fx_ref[start + i + 1, k] = even
                fx_ref[start + i + 2, k] = odd
                left_ref[start + i, k] = left[k]
                left[k] = even + ROOT * left[k]
                left_ref[start + i + 1, k] = left[k]
                left[k] = odd + ROOT * left[k]
                both = ROOT**i * even + ROOT ** (i + 1) * odd
                right[k] = both if i == 0 else right[k] + both
                if i == 0:
                    first[k] = even
                if i == CHUNK - 2:
                    xr_ref[1, k] = odd
                g = fz[k].reshape(2 * width, lanes)
                high = g.astype(jnp.bfloat16)
                low = (g - high.astype(jnp.float32)).astype(jnp.bfloat16)
                at = k * rows + i * width
                high_ref[step, at : at + 2 * width] = high
                low_ref[step, at : at + 2 * width] = low
        for k in range(5):
            xr_ref[0, k] = left[k]
            xl_ref[0, k] = xl_ref[0, k] + w_ref[step, 0] * right[k]
            xl_ref[1, k] = xl_ref[1, k] + w_ref[step, 2] * first[k]
        dims = (((1,), (1,)), ((), ()))
        zw = zw_ref[...]
        one = lax.dot_general(zw, high_ref[step], dims, preferred_element_type=jnp.float32)
        two = lax.dot_general(zw, low_ref[step], dims, preferred_element_type=jnp.float32)
        total = one[0:4] + one[4:8] + two[0:4]
        zr_ref[step] = total[0:2]
        zl_ref[step] = total[2:4]

    def copy_of(n):
        return pltpu.make_async_remote_copy(
            src_ref=pairs[n][0],
            dst_ref=pairs[n][1],
            send_sem=send_sem.at[n],
            recv_sem=recv_sem.at[n],
            device_id=neighbours[n],
            device_id_type=pl.DeviceIdType.MESH,
        )

    @pl.when(step == chunks - 1)
    def _():
        pl.semaphore_wait(barrier, 4)
        for n in range(4):
            copy_of(n).start()

    @pl.when(step >= chunks)
    def _():
        chunk = 2 * chunks - 1 - step
        start = chunk * CHUNK

        @pl.when(step == chunks)
        def _():
            for copy in table_loads():
                copy.wait()

        loads_of(chunk, 3, 4)[0].wait()
        high = high_ref[chunk]
        hh = hh_buf[...]
        dz = jnp.dot(high, hh, preferred_element_type=jnp.float32)
        dz += jnp.dot(low_ref[chunk], hh, preferred_element_type=jnp.float32)
        dz += jnp.dot(high, hl_buf[...], preferred_element_type=jnp.float32)
        dz_ref[...] = dz.reshape(dz_ref.shape)
        right = carry_ref[...]
        upper = fx_ref[start + CHUNK + 1]
        here = fx_ref[start + CHUNK]
        for i in range(CHUNK - 1, -1, -1):
            lower = fx_ref[start + i]
            rate = SUM_COEF * (right - left_ref[start + i]) + DIFF_COEF * (upper - lower)
            part_ref[:, i] = rate + dz_ref[:, i] - (5.0 / 9.0) * reg_buf[:, start + i]
            right = here + ROOT * right
            upper = here
            here = lower
        carry_ref[...] = right

    @pl.when(step == 2 * chunks - 1)
    def _():
        for n in range(4):
            copy_of(n).wait()
        xr_out[...] = xr_got[...]
        xl_out[...] = xl_got[...]
        zr_out[...] = zr_got[...]
        zl_out[...] = zl_got[...]


def final_kernel(
    w_ref, rho_ref, mom_ref, en_ref, part_ref, xr_in, xl_in, zr_in, zl_in, cz_in,
    state_out, out_out, state_ref, out_ref, xr_ref, xl_ref, zr_ref, zl_ref, cz_ref,
    stack_ref, dz_ref, edge_sem, load_sem, store_sem,
):
    chunks = zr_ref.shape[0]
    edges = [
        pltpu.make_async_copy(source, target, edge_sem.at[n])
        for n, (source, target) in enumerate(
            ((xr_in, xr_ref), (xl_in, xl_ref), (zr_in, zr_ref), (zl_in, zl_ref), (cz_in, cz_ref))
        )
    ]
    loads, stores = [], []
    for c in range(chunks):
        at = pl.ds(c * CHUNK, CHUNK)
        ends = (
            (part_ref.at[:, at], out_ref.at[:, at]),
            (rho_ref.at[at], state_ref.at[0, at]),
            (mom_ref.at[:, at], state_ref.at[1:4, at]),
            (en_ref.at[at], state_ref.at[4, at]),
        )
        loads.append([
            pltpu.make_async_copy(source, target, load_sem.at[c, n])
            for n, (source, target) in enumerate(ends)
        ])
        ends = ((out_ref.at[:, at], out_out.at[:, at]), (state_ref.at[:, at], state_out.at[:, at]))
        stores.append([
            pltpu.make_async_copy(source, target, store_sem.at[c, n])
            for n, (source, target) in enumerate(ends)
        ])
    for copy in edges + sum(loads, []):
        copy.start()
    for copy in edges:
        copy.wait()
    stack_ref[12:16] = jnp.zeros((4, stack_ref.shape[1]), jnp.float32)
    for c in range(chunks):
        zr = zr_ref[c]
        zl = zl_ref[c]
        zr_high = zr.astype(jnp.bfloat16).astype(jnp.float32)
        zl_high = zl.astype(jnp.bfloat16).astype(jnp.float32)
        stack_ref[0:2] = zr_high
        stack_ref[2:4] = zl_high
        stack_ref[4:6] = zr - zr_high
        stack_ref[6:8] = zl - zl_high
        stack_ref[8:10] = zr_high
        stack_ref[10:12] = zl_high
        dz = lax.dot_general(
            stack_ref[...].astype(jnp.bfloat16), cz_ref[...], (((0,), (0,)), ((), ())),
            preferred_element_type=jnp.float32,
        )
        dz_ref[...] = dz.reshape(dz_ref.shape)
        left = (-SUM_COEF * w_ref[c, 0]) * xr_ref[0]
        right = (SUM_COEF * w_ref[c, 1]) * xl_ref[0]
        for copy in loads[c]:
            copy.wait()
        for i in range(CHUNK):
            row = c * CHUNK + i
            fresh = out_ref[:, row] + dz_ref[:, i]
            fresh += ROOT**i * left + ROOT ** (CHUNK - 1 - i) * right
            if row == 0:
                fresh -= DIFF_COEF * xr_ref[1]
            if row == chunks * CHUNK - 1:
                fresh += DIFF_COEF * xl_ref[1]
            out_ref[:, row] = fresh
            state_ref[:, row] = state_ref[:, row] + (15.0 / 16.0) * fresh
        for copy in stores[c]:
            copy.start()
    for copy in sum(stores, []):
        copy.wait()


def per_device(density, momentum, energy, register):
    nx, ny, nz = density.shape
    chunks = nx // CHUNK
    rows = CHUNK * ny
    f32, bf16 = jnp.float32, jnp.bfloat16
    table = lambda shape: pl.BlockSpec(shape, lambda c: (0,) * len(shape))
    smem = pl.BlockSpec(memory_space=pltpu.SMEM)
    hbm = pl.BlockSpec(memory_space=pl.ANY)
    weights = jnp.asarray(weight_table(chunks))
    edge_x = (2, 5, ny, nz)
    edge_z = (chunks, 2, 5 * rows)
    buffers = [pltpu.VMEM(edge_x, f32)] * 2 + [pltpu.VMEM(edge_z, f32)] * 2
    high, low = local_table(nz)

    back = lambda s: jnp.minimum(2 * chunks - 1 - s, chunks - 1)
    quint = pl.BlockSpec((5, CHUNK, ny, nz), lambda s: (0, back(s), 0, 0))
    part, xr, xl, zr, zl = pl.pallas_call(
        local_kernel,
        grid=(2 * chunks,),
        in_specs=[
            smem,
            hbm, hbm, hbm, hbm, table((16, nz)), hbm, hbm,
        ],
        out_specs=[quint, table(edge_x), table(edge_x), table(edge_z), table(edge_z)],
        out_shape=[
            jax.ShapeDtypeStruct(shape, f32)
            for shape in ((5, nx, ny, nz), edge_x, edge_x, edge_z, edge_z)
        ],
        scratch_shapes=buffers * 2
        + [
            pltpu.VMEM((nx + 2, 5, ny, nz), f32),
            pltpu.VMEM((nx, 5, ny, nz), f32),
            pltpu.VMEM((chunks, 5 * rows, nz), bf16),
            pltpu.VMEM((chunks, 5 * rows, nz), bf16),
            pltpu.VMEM((5, CHUNK, ny, nz), f32),
            pltpu.VMEM((5, ny, nz), f32),
            pltpu.VMEM((5, nx, ny, nz), f32),
            pltpu.VMEM((5, nx, ny, nz), f32),
            pltpu.VMEM((nz, nz), bf16),
            pltpu.VMEM((nz, nz), bf16),
            pltpu.SemaphoreType.DMA((4,)),
            pltpu.SemaphoreType.DMA((4,)),
            pltpu.SemaphoreType.DMA((chunks, 4)),
            pltpu.SemaphoreType.DMA((2,)),
        ],
        compiler_params=pltpu.CompilerParams(
            dimension_semantics=("arbitrary",),
            vmem_limit_bytes=60 * 1024 * 1024,
            collective_id=0,
            has_side_effects=True,
        ),
        name="local_part",
    )(
        weights, density, momentum, energy, register,
        jnp.asarray(summary_table(nz)), jnp.asarray(high), jnp.asarray(low),
    )

    return pl.pallas_call(
        final_kernel,
        in_specs=[smem] + [hbm] * 9,
        out_specs=[hbm, hbm],
        out_shape=[jax.ShapeDtypeStruct((5, nx, ny, nz), f32)] * 2,
        scratch_shapes=[pltpu.VMEM((5, nx, ny, nz), f32)] * 2
        + buffers
        + [
            pltpu.VMEM((16, nz), bf16),
            pltpu.VMEM((16, 5 * rows), f32),
            pltpu.VMEM((5, CHUNK, ny, nz), f32),
            pltpu.SemaphoreType.DMA((5,)),
            pltpu.SemaphoreType.DMA((chunks, 4)),
            pltpu.SemaphoreType.DMA((chunks, 2)),
        ],
        compiler_params=pltpu.CompilerParams(vmem_limit_bytes=60 * 1024 * 1024),
        name="neighbour_part",
    )(
        weights, density, momentum, energy, part, xr, xl, zr, zl,
        jnp.asarray(correction_table(nz)),
    )


def solution(mesh):
    specs = (
        P("gx", None, "gz"),
        P(None, "gx", None, "gz"),
        P("gx", None, "gz"),
        P(None, "gx", None, "gz"),
    )
    out = P(None, "gx", None, "gz")
    return jax.shard_map(
        per_device, mesh=mesh, in_specs=specs, out_specs=(out, out), check_vma=False
    )
```

```python
import jax
import jax.numpy as jnp
import numpy as np
from jax import lax
from jax.experimental import pallas as pl
from jax.experimental.pallas import tpu as pltpu
from jax.sharding import PartitionSpec as P

ALPHA = 0.45
NEAR = 49.0 / 60.0
FAR = 1.0 / 15.0
STEP = 0.2
CHUNK = 16

ROOT = (np.sqrt(1.0 - 4.0 * ALPHA * ALPHA) - 1.0) / (2.0 * ALPHA)
NORM = 1.0 / np.sqrt(1.0 - 4.0 * ALPHA * ALPHA)
GEOM = NORM * (NEAR * (1.0 / ROOT - ROOT) + FAR * (ROOT**-2 - ROOT**2))
EXTRA = NORM * FAR * (ROOT - 1.0 / ROOT)
SUM_COEF = -STEP * GEOM * ROOT
DIFF_COEF = -STEP * EXTRA


def split(values):
    high = np.asarray(values, np.float32).astype(jnp.bfloat16)
    low = (np.asarray(values, np.float64) - high.astype(np.float64)).astype(jnp.bfloat16)
    return high, low


def summary_table(count):
    cols = np.arange(count)
    rows = np.zeros((4, count))
    rows[0] = ROOT ** (count - 1 - cols)
    rows[1, count - 1] = 1.0
    rows[2] = ROOT**cols
    rows[3, 0] = 1.0
    high, low = split(rows)
    out = np.zeros((16, count), jnp.bfloat16)
    out[0:4] = high
    out[4:8] = low
    return out


def correction_table(count):
    cols = np.arange(count)
    rows = np.zeros((4, count))
    rows[0] = -SUM_COEF * ROOT**cols
    rows[1, 0] = -DIFF_COEF
    rows[2] = SUM_COEF * ROOT ** (count - 1 - cols)
    rows[3, count - 1] = DIFF_COEF
    high, low = split(rows)
    out = np.zeros((16, count), jnp.bfloat16)
    out[0:4] = high
    out[4:8] = high
    out[8:12] = low
    return out


def local_table(count):
    offset = np.arange(count)[:, None] - np.arange(count)[None, :]
    reach = np.abs(offset)
    values = SUM_COEF * np.power(ROOT, np.maximum(reach - 1, 0)) + DIFF_COEF * (reach == 1)
    return split(np.sign(offset) * values)


def fluxes(rho, mx, my, mz, energy):
    inverse = 1.0 / rho
    vx = mx * inverse
    vz = mz * inverse
    pressure = 0.4 * (energy - 0.5 * (mx * mx + my * my + mz * mz) * inverse)
    total = energy + pressure
    fx = (mx, mx * vx + pressure, my * vx, mz * vx, total * vx)
    fz = (mz, mx * vz, my * vz, mz * vz + pressure, total * vz)
    return fx, fz


def local_kernel(
    rho_ref, mom_ref, en_ref, reg_ref, zw_ref, hh_ref, hl_ref, cz_ref,
    part_ref, cell_ref, xr_out, xl_out, zr_out, zl_out, cz_out,
    xr_ref, xl_ref, zr_ref, zl_ref, xr_got, xl_got, zr_got, zl_got,
    fx_ref, left_ref, high_ref, low_ref, dz_ref, carry_ref,
    reg_buf, hh_buf, hl_buf, zw_buf, send_sem, recv_sem, load_sem, table_sem,
):
    chunks = high_ref.shape[0]
    cells, width, lanes = fx_ref.shape[0] - 2, fx_ref.shape[2], fx_ref.shape[3]
    rows = CHUNK * width
    gx, gz = lax.axis_index("gx"), lax.axis_index("gz")
    nx, nz = lax.axis_size("gx"), lax.axis_size("gz")
    x_next, x_prev = lax.rem(gx + 1, nx), lax.rem(gx + nx - 1, nx)
    z_next, z_prev = lax.rem(gz + 1, nz), lax.rem(gz + nz - 1, nz)
    neighbours = ((x_next, gz), (x_prev, gz), (gx, z_next), (gx, z_prev))
    barrier = pltpu.get_barrier_semaphore()
    pairs = ((xr_ref, xr_got), (xl_ref, xl_got), (zr_ref, zr_got), (zl_ref, zl_got))

    def loads_of(chunk, first, stop):
        at = pl.ds(chunk * CHUNK, CHUNK)
        ends = (
            (rho_ref.at[at], cell_ref.at[0, at]),
            (mom_ref.at[:, at], cell_ref.at[1:4, at]),
            (en_ref.at[at], cell_ref.at[4, at]),
            (reg_ref.at[:, at], reg_buf.at[:, at]),
        )
        return [
            pltpu.make_async_copy(source, target, load_sem.at[chunk, n])
            for n, (source, target) in enumerate(ends)
            if first <= n < stop
        ]

    def table_loads():
        return (
            pltpu.make_async_copy(hh_ref, hh_buf, table_sem.at[0]),
            pltpu.make_async_copy(hl_ref, hl_buf, table_sem.at[1]),
            pltpu.make_async_copy(cz_ref, cz_out, table_sem.at[2]),
        )

    zw_load = pltpu.make_async_copy(zw_ref, zw_buf, table_sem.at[3])

    def enter():
        for chunk in range(chunks):
            for copy in loads_of(chunk, 0, 3):
                copy.start()
        zw_load.start()
        for copy in table_loads():
            copy.start()
        for chunk in range(chunks - 1, -1, -1):
            loads_of(chunk, 3, 4)[0].start()
        for target in neighbours:
            pl.semaphore_signal(
                barrier, inc=1, device_id=target, device_id_type=pl.DeviceIdType.MESH
            )
        xr_ref[...] = jnp.zeros_like(xr_ref)
        xl_ref[...] = jnp.zeros_like(xl_ref)
        carry_ref[...] = jnp.zeros_like(carry_ref)
        fx_ref[0] = jnp.zeros((5, width, lanes), jnp.float32)
        fx_ref[cells + 1] = jnp.zeros((5, width, lanes), jnp.float32)

    def forward(step, weight):
        start = step * CHUNK
        for copy in loads_of(step, 0, 3):
            copy.wait()
        left = [xr_ref[0, k] for k in range(5)]
        right = [None] * 5
        first = [None] * 5
        for i in range(0, CHUNK, 2):
            fx, fz = fluxes(*(cell_ref[k, pl.ds(start + i, 2)] for k in range(5)))
            for k in range(5):
                even, odd = fx[k][0], fx[k][1]
                fx_ref[start + i + 1, k] = even
                fx_ref[start + i + 2, k] = odd
                left_ref[start + i, k] = left[k]
                left[k] = even + ROOT * left[k]
                left_ref[start + i + 1, k] = left[k]
                left[k] = odd + ROOT * left[k]
                both = ROOT**i * even + ROOT ** (i + 1) * odd
                right[k] = both if i == 0 else right[k] + both
                if i == 0:
                    first[k] = even
                if i == CHUNK - 2:
                    xr_ref[1, k] = odd
                g = fz[k].reshape(2 * width, lanes)
                high = g.astype(jnp.bfloat16)
                low = (g - high.astype(jnp.float32)).astype(jnp.bfloat16)
                at = k * rows + i * width
                high_ref[step, at : at + 2 * width] = high
                low_ref[step, at : at + 2 * width] = low
        for k in range(5):
            xr_ref[0, k] = left[k]
            xl_ref[0, k] = xl_ref[0, k] + weight * right[k]
            xl_ref[1, k] = xl_ref[1, k] + jnp.where(step == 0, 1.0, 0.0) * first[k]
        dims = (((1,), (1,)), ((), ()))
        zw = zw_buf[...]
        one = lax.dot_general(zw, high_ref[step], dims, preferred_element_type=jnp.float32)
        two = lax.dot_general(zw, low_ref[step], dims, preferred_element_type=jnp.float32)
        total = one[0:4] + one[4:8] + two[0:4]
        zr_ref[step] = total[0:2]
        zl_ref[step] = total[2:4]
        return weight * (ROOT**CHUNK)

    def copy_of(n):
        return pltpu.make_async_remote_copy(
            src_ref=pairs[n][0],
            dst_ref=pairs[n][1],
            send_sem=send_sem.at[n],
            recv_sem=recv_sem.at[n],
            device_id=neighbours[n],
            device_id_type=pl.DeviceIdType.MESH,
        )

    def send():
        pl.semaphore_wait(barrier, 4)
        for n in range(4):
            copy_of(n).start()

    def backward(step, none):
        chunk = 2 * chunks - 1 - step
        start = chunk * CHUNK

        loads_of(chunk, 3, 4)[0].wait()
        high = high_ref[chunk]
        hh = hh_buf[...]
        dz = jnp.dot(high, hh, preferred_element_type=jnp.float32)
        dz += jnp.dot(low_ref[chunk], hh, preferred_element_type=jnp.float32)
        dz += jnp.dot(high, hl_buf[...], preferred_element_type=jnp.float32)
        dz_ref[...] = dz.reshape(dz_ref.shape)
        right = carry_ref[...]
        upper = fx_ref[start + CHUNK + 1]
        here = fx_ref[start + CHUNK]
        for i in range(CHUNK - 1, -1, -1):
            lower = fx_ref[start + i]
            rate = SUM_COEF * (right - left_ref[start + i]) + DIFF_COEF * (upper - lower)
            part_ref[:, start + i] = rate + dz_ref[:, i] - (5.0 / 9.0) * reg_buf[:, start + i]
            right = here + ROOT * right
            upper = here
            here = lower
        carry_ref[...] = right
        return none

    enter()
    zw_load.wait()
    lax.fori_loop(0, chunks, forward, jnp.float32(1.0))
    send()
    for copy in table_loads():
        copy.wait()
    lax.fori_loop(chunks, 2 * chunks, backward, 0)
    for n in range(4):
        copy_of(n).wait()
    xr_out[...] = xr_got[...]
    xl_out[...] = xl_got[...]
    zr_out[...] = zr_got[...]
    zl_out[...] = zl_got[...]


def final_kernel(
    part_ref, cell_ref, xr_ref, xl_ref, zr_ref, zl_ref, cz_ref,
    state_out, out_out, state_ref, out_ref, stack_ref, dz_ref, store_sem,
):
    chunks = zr_ref.shape[0]
    stores = []
    for c in range(chunks):
        at = pl.ds(c * CHUNK, CHUNK)
        ends = ((out_ref.at[:, at], out_out.at[:, at]), (state_ref.at[:, at], state_out.at[:, at]))
        stores.append([
            pltpu.make_async_copy(source, target, store_sem.at[c, n])
            for n, (source, target) in enumerate(ends)
        ])
    stack_ref[12:16] = jnp.zeros((4, stack_ref.shape[1]), jnp.float32)
    for c in range(chunks):
        zr = zr_ref[c]
        zl = zl_ref[c]
        zr_high = zr.astype(jnp.bfloat16).astype(jnp.float32)
        zl_high = zl.astype(jnp.bfloat16).astype(jnp.float32)
        stack_ref[0:2] = zr_high
        stack_ref[2:4] = zl_high
        stack_ref[4:6] = zr - zr_high
        stack_ref[6:8] = zl - zl_high
        stack_ref[8:10] = zr_high
        stack_ref[10:12] = zl_high
        dz = lax.dot_general(
            stack_ref[...].astype(jnp.bfloat16), cz_ref[...], (((0,), (0,)), ((), ())),
            preferred_element_type=jnp.float32,
        )
        dz_ref[...] = dz.reshape(dz_ref.shape)
        left = (-SUM_COEF * ROOT ** (c * CHUNK)) * xr_ref[0]
        right = (SUM_COEF * ROOT ** ((chunks - 1 - c) * CHUNK)) * xl_ref[0]
        for i in range(CHUNK):
            row = c * CHUNK + i
            fresh = part_ref[:, row] + dz_ref[:, i]
            fresh += ROOT**i * left + ROOT ** (CHUNK - 1 - i) * right
            if row == 0:
                fresh -= DIFF_COEF * xr_ref[1]
            if row == chunks * CHUNK - 1:
                fresh += DIFF_COEF * xl_ref[1]
            out_ref[:, row] = fresh
            state_ref[:, row] = cell_ref[:, row] + (15.0 / 16.0) * fresh
        for copy in stores[c]:
            copy.start()
    for copy in sum(stores, []):
        copy.wait()


def per_device(density, momentum, energy, register):
    nx, ny, nz = density.shape
    chunks = nx // CHUNK
    rows = CHUNK * ny
    f32, bf16 = jnp.float32, jnp.bfloat16
    vmem = pl.BlockSpec(memory_space=pltpu.VMEM)
    hbm = pl.BlockSpec(memory_space=pl.ANY)
    far = lambda value: pltpu.with_memory_space_constraint(value, pltpu.HBM)
    close = lambda value: pltpu.with_memory_space_constraint(value, pltpu.VMEM)
    edge_x = (2, 5, ny, nz)
    edge_z = (chunks, 2, 5 * rows)
    full = (5, nx, ny, nz)
    buffers = [pltpu.VMEM(edge_x, f32)] * 2 + [pltpu.VMEM(edge_z, f32)] * 2
    high, low = local_table(nz)

    kept = pl.pallas_call(
        local_kernel,
        in_specs=[hbm] * 8,
        out_specs=[vmem] * 7,
        out_shape=[
            pltpu.VMEM(shape, f32) for shape in (full, full, edge_x, edge_x, edge_z, edge_z)
        ]
        + [pltpu.VMEM((16, nz), bf16)],
        scratch_shapes=buffers * 2
        + [
            pltpu.VMEM((nx + 2, 5, ny, nz), f32),
            pltpu.VMEM((nx, 5, ny, nz), f32),
            pltpu.VMEM((chunks, 5 * rows, nz), bf16),
            pltpu.VMEM((chunks, 5 * rows, nz), bf16),
            pltpu.VMEM((5, CHUNK, ny, nz), f32),
            pltpu.VMEM((5, ny, nz), f32),
            pltpu.VMEM(full, f32),
            pltpu.VMEM((nz, nz), bf16),
            pltpu.VMEM((nz, nz), bf16),
            pltpu.VMEM((16, nz), bf16),
            pltpu.SemaphoreType.DMA((4,)),
            pltpu.SemaphoreType.DMA((4,)),
            pltpu.SemaphoreType.DMA((chunks, 4)),
            pltpu.SemaphoreType.DMA((4,)),
        ],
        compiler_params=pltpu.CompilerParams(
            vmem_limit_bytes=36 * 1024 * 1024, collective_id=0, has_side_effects=True
        ),
        name="local_part",
    )(
        far(density), far(momentum), far(energy), far(register),
        far(jnp.asarray(summary_table(nz))), far(jnp.asarray(high)), far(jnp.asarray(low)),
        far(jnp.asarray(correction_table(nz))),
    )

    return pl.pallas_call(
        final_kernel,
        in_specs=[vmem] * 7,
        out_specs=[hbm, hbm],
        out_shape=[jax.ShapeDtypeStruct(full, f32)] * 2,
        scratch_shapes=[pltpu.VMEM(full, f32)] * 2
        + [
            pltpu.VMEM((16, 5 * rows), f32),
            pltpu.VMEM((5, CHUNK, ny, nz), f32),
            pltpu.SemaphoreType.DMA((chunks, 2)),
        ],
        compiler_params=pltpu.CompilerParams(vmem_limit_bytes=36 * 1024 * 1024),
        name="neighbour_part",
    )(*(close(value) for value in kept))


def solution(mesh):
    specs = (
        P("gx", None, "gz"),
        P(None, "gx", None, "gz"),
        P("gx", None, "gz"),
        P(None, "gx", None, "gz"),
    )
    out = P(None, "gx", None, "gz")
    return jax.shard_map(
        per_device, mesh=mesh, in_specs=specs, out_specs=(out, out), check_vma=False
    )
```

```python
import jax
import jax.numpy as jnp
import numpy as np
from jax import lax
from jax.experimental import pallas as pl
from jax.experimental.pallas import tpu as pltpu
from jax.sharding import PartitionSpec as P

ALPHA = 0.45
NEAR = 49.0 / 60.0
FAR = 1.0 / 15.0
STEP = 0.2
CHUNK = 16

ROOT = (np.sqrt(1.0 - 4.0 * ALPHA * ALPHA) - 1.0) / (2.0 * ALPHA)
NORM = 1.0 / np.sqrt(1.0 - 4.0 * ALPHA * ALPHA)
GEOM = NORM * (NEAR * (1.0 / ROOT - ROOT) + FAR * (ROOT**-2 - ROOT**2))
EXTRA = NORM * FAR * (ROOT - 1.0 / ROOT)
SUM_COEF = -STEP * GEOM * ROOT
DIFF_COEF = -STEP * EXTRA


def split(values):
    high = np.asarray(values, np.float32).astype(jnp.bfloat16)
    low = (np.asarray(values, np.float64) - high.astype(np.float64)).astype(jnp.bfloat16)
    return high, low


def summary_table(count):
    cols = np.arange(count)
    rows = np.zeros((4, count))
    rows[0] = ROOT ** (count - 1 - cols)
    rows[1, count - 1] = 1.0
    rows[2] = ROOT**cols
    rows[3, 0] = 1.0
    high, low = split(rows)
    out = np.zeros((16, count), jnp.bfloat16)
    out[0:4] = high
    out[4:8] = low
    return out


def correction_table(count):
    cols = np.arange(count)
    rows = np.zeros((4, count))
    rows[0] = -SUM_COEF * ROOT**cols
    rows[1, 0] = -DIFF_COEF
    rows[2] = SUM_COEF * ROOT ** (count - 1 - cols)
    rows[3, count - 1] = DIFF_COEF
    high, low = split(rows)
    out = np.zeros((16, count), jnp.bfloat16)
    out[0:4] = high
    out[4:8] = high
    out[8:12] = low
    return out


def local_table(count):
    offset = np.arange(count)[:, None] - np.arange(count)[None, :]
    reach = np.abs(offset)
    values = SUM_COEF * np.power(ROOT, np.maximum(reach - 1, 0)) + DIFF_COEF * (reach == 1)
    return split(np.sign(offset) * values)


def fluxes(rho, mx, my, mz, energy):
    inverse = 1.0 / rho
    vx = mx * inverse
    vz = mz * inverse
    pressure = 0.4 * (energy - 0.5 * (mx * mx + my * my + mz * mz) * inverse)
    total = energy + pressure
    fx = (mx, mx * vx + pressure, my * vx, mz * vx, total * vx)
    fz = (mz, mx * vz, my * vz, mz * vz + pressure, total * vz)
    return fx, fz


def local_kernel(
    rho_ref, mom_ref, en_ref, reg_ref, zw_ref, hh_ref, hl_ref, cz_ref,
    part_ref, cell_ref, xr_out, xl_out, zr_out, zl_out, cz_out,
    xr_ref, xl_ref, zr_ref, zl_ref, xr_got, xl_got, zr_got, zl_got,
    fx_ref, left_ref, high_ref, low_ref, dz_ref, carry_ref,
    reg_buf, hh_buf, hl_buf, zw_buf, send_sem, recv_sem, load_sem, table_sem,
):
    chunks = high_ref.shape[0]
    cells, width, lanes = fx_ref.shape[0] - 2, fx_ref.shape[2], fx_ref.shape[3]
    rows = CHUNK * width
    gx, gz = lax.axis_index("gx"), lax.axis_index("gz")
    nx, nz = lax.axis_size("gx"), lax.axis_size("gz")
    x_next, x_prev = lax.rem(gx + 1, nx), lax.rem(gx + nx - 1, nx)
    z_next, z_prev = lax.rem(gz + 1, nz), lax.rem(gz + nz - 1, nz)
    neighbours = ((x_next, gz), (x_prev, gz), (gx, z_next), (gx, z_prev))
    barrier = pltpu.get_barrier_semaphore()
    pairs = ((xr_ref, xr_got), (xl_ref, xl_got), (zr_ref, zr_got), (zl_ref, zl_got))

    def loads_of(chunk, first, stop):
        at = pl.ds(chunk * CHUNK, CHUNK)
        ends = (
            (rho_ref.at[at], cell_ref.at[0, at]),
            (mom_ref.at[:, at], cell_ref.at[1:4, at]),
            (en_ref.at[at], cell_ref.at[4, at]),
            (reg_ref.at[:, at], reg_buf.at[:, at]),
        )
        return [
            pltpu.make_async_copy(source, target, load_sem.at[chunk, n])
            for n, (source, target) in enumerate(ends)
            if first <= n < stop
        ]

    def table_loads():
        return (
            pltpu.make_async_copy(hh_ref, hh_buf, table_sem.at[0]),
            pltpu.make_async_copy(hl_ref, hl_buf, table_sem.at[1]),
            pltpu.make_async_copy(cz_ref, cz_out, table_sem.at[2]),
        )

    zw_load = pltpu.make_async_copy(zw_ref, zw_buf, table_sem.at[3])

    def enter():
        for chunk in range(chunks):
            for copy in loads_of(chunk, 0, 3):
                copy.start()
        zw_load.start()
        for target in neighbours:
            pl.semaphore_signal(
                barrier, inc=1, device_id=target, device_id_type=pl.DeviceIdType.MESH
            )
        xr_ref[...] = jnp.zeros_like(xr_ref)
        xl_ref[...] = jnp.zeros_like(xl_ref)
        carry_ref[...] = jnp.zeros_like(carry_ref)
        fx_ref[0] = jnp.zeros((5, width, lanes), jnp.float32)
        fx_ref[cells + 1] = jnp.zeros((5, width, lanes), jnp.float32)

    def forward(step, weight):
        start = step * CHUNK
        for copy in loads_of(step, 0, 3):
            copy.wait()

        @pl.when(step == chunks // 2)
        def _():
            for copy in table_loads():
                copy.start()
            for chunk in range(chunks - 1, -1, -1):
                loads_of(chunk, 3, 4)[0].start()

        left = [xr_ref[0, k] for k in range(5)]
        right = [None] * 5
        first = [None] * 5
        for i in range(0, CHUNK, 2):
            fx, fz = fluxes(*(cell_ref[k, pl.ds(start + i, 2)] for k in range(5)))
            for k in range(5):
                even, odd = fx[k][0], fx[k][1]
                fx_ref[start + i + 1, k] = even
                fx_ref[start + i + 2, k] = odd
                left_ref[start + i, k] = left[k]
                left[k] = even + ROOT * left[k]
                left_ref[start + i + 1, k] = left[k]
                left[k] = odd + ROOT * left[k]
                both = ROOT**i * even + ROOT ** (i + 1) * odd
                right[k] = both if i == 0 else right[k] + both
                if i == 0:
                    first[k] = even
                if i == CHUNK - 2:
                    xr_ref[1, k] = odd
                g = fz[k].reshape(2 * width, lanes)
                high = g.astype(jnp.bfloat16)
                low = (g - high.astype(jnp.float32)).astype(jnp.bfloat16)
                at = k * rows + i * width
                high_ref[step, at : at + 2 * width] = high
                low_ref[step, at : at + 2 * width] = low
        for k in range(5):
            xr_ref[0, k] = left[k]
            xl_ref[0, k] = xl_ref[0, k] + weight * right[k]
            xl_ref[1, k] = xl_ref[1, k] + jnp.where(step == 0, 1.0, 0.0) * first[k]
        dims = (((1,), (1,)), ((), ()))
        zw = zw_buf[...]
        one = lax.dot_general(zw, high_ref[step], dims, preferred_element_type=jnp.float32)
        two = lax.dot_general(zw, low_ref[step], dims, preferred_element_type=jnp.float32)
        total = one[0:4] + one[4:8] + two[0:4]
        zr_ref[step] = total[0:2]
        zl_ref[step] = total[2:4]
        return weight * (ROOT**CHUNK)

    def copy_of(n):
        return pltpu.make_async_remote_copy(
            src_ref=pairs[n][0],
            dst_ref=pairs[n][1],
            send_sem=send_sem.at[n],
            recv_sem=recv_sem.at[n],
            device_id=neighbours[n],
            device_id_type=pl.DeviceIdType.MESH,
        )

    def send():
        pl.semaphore_wait(barrier, 4)
        for n in range(4):
            copy_of(n).start()

    def backward(step, none):
        chunk = 2 * chunks - 1 - step
        start = chunk * CHUNK

        loads_of(chunk, 3, 4)[0].wait()
        high = high_ref[chunk]
        hh = hh_buf[...]
        dz = jnp.dot(high, hh, preferred_element_type=jnp.float32)
        dz += jnp.dot(low_ref[chunk], hh, preferred_element_type=jnp.float32)
        dz += jnp.dot(high, hl_buf[...], preferred_element_type=jnp.float32)
        dz_ref[...] = dz.reshape(dz_ref.shape)
        right = carry_ref[...]
        upper = fx_ref[start + CHUNK + 1]
        here = fx_ref[start + CHUNK]
        for i in range(CHUNK - 1, -1, -1):
            lower = fx_ref[start + i]
            rate = SUM_COEF * (right - left_ref[start + i]) + DIFF_COEF * (upper - lower)
            part_ref[:, start + i] = rate + dz_ref[:, i] - (5.0 / 9.0) * reg_buf[:, start + i]
            right = here + ROOT * right
            upper = here
            here = lower
        carry_ref[...] = right
        return none

    enter()
    zw_load.wait()
    lax.fori_loop(0, chunks, forward, jnp.float32(1.0))
    send()
    for copy in table_loads():
        copy.wait()
    lax.fori_loop(chunks, 2 * chunks, backward, 0)
    for n in range(4):
        copy_of(n).wait()
    xr_out[...] = xr_got[...]
    xl_out[...] = xl_got[...]
    zr_out[...] = zr_got[...]
    zl_out[...] = zl_got[...]


def final_kernel(
    part_ref, cell_ref, xr_ref, xl_ref, zr_ref, zl_ref, cz_ref,
    state_out, out_out, state_ref, out_ref, stack_ref, dz_ref, store_sem,
):
    chunks = zr_ref.shape[0]
    stores = []
    for c in range(chunks):
        at = pl.ds(c * CHUNK, CHUNK)
        ends = ((out_ref.at[:, at], out_out.at[:, at]), (state_ref.at[:, at], state_out.at[:, at]))
        stores.append([
            pltpu.make_async_copy(source, target, store_sem.at[c, n])
            for n, (source, target) in enumerate(ends)
        ])
    stack_ref[12:16] = jnp.zeros((4, stack_ref.shape[1]), jnp.float32)
    for c in range(chunks):
        zr = zr_ref[c]
        zl = zl_ref[c]
        zr_high = zr.astype(jnp.bfloat16).astype(jnp.float32)
        zl_high = zl.astype(jnp.bfloat16).astype(jnp.float32)
        stack_ref[0:2] = zr_high
        stack_ref[2:4] = zl_high
        stack_ref[4:6] = zr - zr_high
        stack_ref[6:8] = zl - zl_high
        stack_ref[8:10] = zr_high
        stack_ref[10:12] = zl_high
        dz = lax.dot_general(
            stack_ref[...].astype(jnp.bfloat16), cz_ref[...], (((0,), (0,)), ((), ())),
            preferred_element_type=jnp.float32,
        )
        dz_ref[...] = dz.reshape(dz_ref.shape)
        left = (-SUM_COEF * ROOT ** (c * CHUNK)) * xr_ref[0]
        right = (SUM_COEF * ROOT ** ((chunks - 1 - c) * CHUNK)) * xl_ref[0]
        for i in range(CHUNK):
            row = c * CHUNK + i
            fresh = part_ref[:, row] + dz_ref[:, i]
            fresh += ROOT**i * left + ROOT ** (CHUNK - 1 - i) * right
            if row == 0:
                fresh -= DIFF_COEF * xr_ref[1]
            if row == chunks * CHUNK - 1:
                fresh += DIFF_COEF * xl_ref[1]
            out_ref[:, row] = fresh
            state_ref[:, row] = cell_ref[:, row] + (15.0 / 16.0) * fresh
        for copy in stores[c]:
            copy.start()
    for copy in sum(stores, []):
        copy.wait()


def per_device(density, momentum, energy, register):
    nx, ny, nz = density.shape
    chunks = nx // CHUNK
    rows = CHUNK * ny
    f32, bf16 = jnp.float32, jnp.bfloat16
    vmem = pl.BlockSpec(memory_space=pltpu.VMEM)
    hbm = pl.BlockSpec(memory_space=pl.ANY)
    far = lambda value: pltpu.with_memory_space_constraint(value, pltpu.HBM)
    close = lambda value: pltpu.with_memory_space_constraint(value, pltpu.VMEM)
    edge_x = (2, 5, ny, nz)
    edge_z = (chunks, 2, 5 * rows)
    full = (5, nx, ny, nz)
    buffers = [pltpu.VMEM(edge_x, f32)] * 2 + [pltpu.VMEM(edge_z, f32)] * 2
    high, low = local_table(nz)

    kept = pl.pallas_call(
        local_kernel,
        in_specs=[hbm] * 8,
        out_specs=[vmem] * 7,
        out_shape=[
            pltpu.VMEM(shape, f32) for shape in (full, full, edge_x, edge_x, edge_z, edge_z)
        ]
        + [pltpu.VMEM((16, nz), bf16)],
        scratch_shapes=buffers * 2
        + [
            pltpu.VMEM((nx + 2, 5, ny, nz), f32),
            pltpu.VMEM((nx, 5, ny, nz), f32),
            pltpu.VMEM((chunks, 5 * rows, nz), bf16),
            pltpu.VMEM((chunks, 5 * rows, nz), bf16),
            pltpu.VMEM((5, CHUNK, ny, nz), f32),
            pltpu.VMEM((5, ny, nz), f32),
            pltpu.VMEM(full, f32),
            pltpu.VMEM((nz, nz), bf16),
            pltpu.VMEM((nz, nz), bf16),
            pltpu.VMEM((16, nz), bf16),
            pltpu.SemaphoreType.DMA((4,)),
            pltpu.SemaphoreType.DMA((4,)),
            pltpu.SemaphoreType.DMA((chunks, 4)),
            pltpu.SemaphoreType.DMA((4,)),
        ],
        compiler_params=pltpu.CompilerParams(
            vmem_limit_bytes=36 * 1024 * 1024, collective_id=0, has_side_effects=True
        ),
        name="local_part",
    )(
        far(density), far(momentum), far(energy), far(register),
        far(jnp.asarray(summary_table(nz))), far(jnp.asarray(high)), far(jnp.asarray(low)),
        far(jnp.asarray(correction_table(nz))),
    )

    return pl.pallas_call(
        final_kernel,
        in_specs=[vmem] * 7,
        out_specs=[hbm, hbm],
        out_shape=[jax.ShapeDtypeStruct(full, f32)] * 2,
        scratch_shapes=[pltpu.VMEM(full, f32)] * 2
        + [
            pltpu.VMEM((16, 5 * rows), f32),
            pltpu.VMEM((5, CHUNK, ny, nz), f32),
            pltpu.SemaphoreType.DMA((chunks, 2)),
        ],
        compiler_params=pltpu.CompilerParams(vmem_limit_bytes=36 * 1024 * 1024),
        name="neighbour_part",
    )(*(close(value) for value in kept))


def solution(mesh):
    specs = (
        P("gx", None, "gz"),
        P(None, "gx", None, "gz"),
        P("gx", None, "gz"),
        P(None, "gx", None, "gz"),
    )
    out = P(None, "gx", None, "gz")
    return jax.shard_map(
        per_device, mesh=mesh, in_specs=specs, out_specs=(out, out), check_vma=False
    )
```

```python
import jax
import jax.numpy as jnp
import numpy as np
from jax import lax
from jax.experimental import pallas as pl
from jax.experimental.pallas import tpu as pltpu
from jax.sharding import PartitionSpec as P

ALPHA = 0.45
NEAR = 49.0 / 60.0
FAR = 1.0 / 15.0
STEP = 0.2
CHUNK = 16

ROOT = (np.sqrt(1.0 - 4.0 * ALPHA * ALPHA) - 1.0) / (2.0 * ALPHA)
NORM = 1.0 / np.sqrt(1.0 - 4.0 * ALPHA * ALPHA)
GEOM = NORM * (NEAR * (1.0 / ROOT - ROOT) + FAR * (ROOT**-2 - ROOT**2))
EXTRA = NORM * FAR * (ROOT - 1.0 / ROOT)
SUM_COEF = -STEP * GEOM * ROOT
DIFF_COEF = -STEP * EXTRA


def split(values):
    high = np.asarray(values, np.float32).astype(jnp.bfloat16)
    low = (np.asarray(values, np.float64) - high.astype(np.float64)).astype(jnp.bfloat16)
    return high, low


def summary_table(count):
    cols = np.arange(count)
    rows = np.zeros((4, count))
    rows[0] = ROOT ** (count - 1 - cols)
    rows[1, count - 1] = 1.0
    rows[2] = ROOT**cols
    rows[3, 0] = 1.0
    high, low = split(rows)
    out = np.zeros((16, count), jnp.bfloat16)
    out[0:4] = high
    out[4:8] = low
    return out


def correction_table(count):
    cols = np.arange(count)
    rows = np.zeros((4, count))
    rows[0] = -SUM_COEF * ROOT**cols
    rows[1, 0] = -DIFF_COEF
    rows[2] = SUM_COEF * ROOT ** (count - 1 - cols)
    rows[3, count - 1] = DIFF_COEF
    high, low = split(rows)
    out = np.zeros((16, count), jnp.bfloat16)
    out[0:4] = high
    out[4:8] = high
    out[8:12] = low
    return out


def local_table(count):
    offset = np.arange(count)[:, None] - np.arange(count)[None, :]
    reach = np.abs(offset)
    values = SUM_COEF * np.power(ROOT, np.maximum(reach - 1, 0)) + DIFF_COEF * (reach == 1)
    return split(np.sign(offset) * values)


def fluxes(rho, mx, my, mz, energy):
    inverse = 1.0 / rho
    vx = mx * inverse
    vz = mz * inverse
    pressure = 0.4 * (energy - 0.5 * (mx * mx + my * my + mz * mz) * inverse)
    total = energy + pressure
    fx = (mx, mx * vx + pressure, my * vx, mz * vx, total * vx)
    fz = (mz, mx * vz, my * vz, mz * vz + pressure, total * vz)
    return fx, fz


def local_kernel(
    rho_ref, mom_ref, en_ref, reg_ref, zw_ref, hh_ref, hl_ref, cz_ref,
    part_ref, cell_ref, xr_out, xl_out, zr_out, zl_out, cz_out,
    xr_ref, xl_ref, zr_ref, zl_ref, xr_got, xl_got, zr_got, zl_got,
    fx_ref, left_ref, high_ref, low_ref, dz_ref, carry_ref,
    reg_buf, hh_buf, hl_buf, zw_buf, send_sem, recv_sem, load_sem, table_sem,
):
    chunks = high_ref.shape[0]
    cells, width, lanes = fx_ref.shape[0] - 2, fx_ref.shape[2], fx_ref.shape[3]
    rows = CHUNK * width
    gx, gz = lax.axis_index("gx"), lax.axis_index("gz")
    nx, nz = lax.axis_size("gx"), lax.axis_size("gz")
    x_next, x_prev = lax.rem(gx + 1, nx), lax.rem(gx + nx - 1, nx)
    z_next, z_prev = lax.rem(gz + 1, nz), lax.rem(gz + nz - 1, nz)
    neighbours = ((x_next, gz), (x_prev, gz), (gx, z_next), (gx, z_prev))
    barrier = pltpu.get_barrier_semaphore()
    pairs = ((xr_ref, xr_got), (xl_ref, xl_got), (zr_ref, zr_got), (zl_ref, zl_got))

    def loads_of(chunk, first, stop):
        at = pl.ds(chunk * CHUNK, CHUNK)
        ends = (
            (rho_ref.at[at], cell_ref.at[0, at]),
            (mom_ref.at[:, at], cell_ref.at[1:4, at]),
            (en_ref.at[at], cell_ref.at[4, at]),
            (reg_ref.at[:, at], reg_buf.at[:, at]),
        )
        return [
            pltpu.make_async_copy(source, target, load_sem.at[chunk, n])
            for n, (source, target) in enumerate(ends)
            if first <= n < stop
        ]

    def table_loads():
        return (
            pltpu.make_async_copy(hh_ref, hh_buf, table_sem.at[0]),
            pltpu.make_async_copy(hl_ref, hl_buf, table_sem.at[1]),
            pltpu.make_async_copy(cz_ref, cz_out, table_sem.at[2]),
        )

    zw_load = pltpu.make_async_copy(zw_ref, zw_buf, table_sem.at[3])

    def enter():
        for chunk in range(chunks):
            for copy in loads_of(chunk, 0, 3):
                copy.start()
        zw_load.start()
        for copy in table_loads():
            copy.start()
        for chunk in range(chunks - 1, -1, -1):
            loads_of(chunk, 3, 4)[0].start()
        for target in neighbours:
            pl.semaphore_signal(
                barrier, inc=1, device_id=target, device_id_type=pl.DeviceIdType.MESH
            )
        xr_ref[...] = jnp.zeros_like(xr_ref)
        xl_ref[...] = jnp.zeros_like(xl_ref)
        carry_ref[...] = jnp.zeros_like(carry_ref)
        fx_ref[0] = jnp.zeros((5, width, lanes), jnp.float32)
        fx_ref[cells + 1] = jnp.zeros((5, width, lanes), jnp.float32)

    def forward(step, weight):
        start = step * CHUNK
        for copy in loads_of(step, 0, 3):
            copy.wait()
        left = [xr_ref[0, k] for k in range(5)]
        right = [None] * 5
        first = [None] * 5
        for i in range(0, CHUNK, 2):
            fx, fz = fluxes(*(cell_ref[k, pl.ds(start + i, 2)] for k in range(5)))
            for k in range(5):
                even, odd = fx[k][0], fx[k][1]
                fx_ref[start + i + 1, k] = even
                fx_ref[start + i + 2, k] = odd
                left_ref[start + i, k] = left[k]
                left[k] = even + ROOT * left[k]
                left_ref[start + i + 1, k] = left[k]
                left[k] = odd + ROOT * left[k]
                both = ROOT**i * even + ROOT ** (i + 1) * odd
                right[k] = both if i == 0 else right[k] + both
                if i == 0:
                    first[k] = even
                if i == CHUNK - 2:
                    xr_ref[1, k] = odd
                g = fz[k].reshape(2 * width, lanes)
                high = g.astype(jnp.bfloat16)
                low = (g - high.astype(jnp.float32)).astype(jnp.bfloat16)
                at = k * rows + i * width
                high_ref[step, at : at + 2 * width] = high
                low_ref[step, at : at + 2 * width] = low
        for k in range(5):
            xr_ref[0, k] = left[k]
            xl_ref[0, k] = xl_ref[0, k] + weight * right[k]
            xl_ref[1, k] = xl_ref[1, k] + jnp.where(step == 0, 1.0, 0.0) * first[k]
        dims = (((1,), (1,)), ((), ()))
        zw = zw_buf[...]
        one = lax.dot_general(zw, high_ref[step], dims, preferred_element_type=jnp.float32)
        two = lax.dot_general(zw, low_ref[step], dims, preferred_element_type=jnp.float32)
        total = one[0:4] + one[4:8] + two[0:4]
        zr_ref[step] = total[0:2]
        zl_ref[step] = total[2:4]
        return weight * (ROOT**CHUNK)

    def copy_of(n):
        return pltpu.make_async_remote_copy(
            src_ref=pairs[n][0],
            dst_ref=pairs[n][1],
            send_sem=send_sem.at[n],
            recv_sem=recv_sem.at[n],
            device_id=neighbours[n],
            device_id_type=pl.DeviceIdType.MESH,
        )

    def send():
        pl.semaphore_wait(barrier, 4)
        for n in range(4):
            copy_of(n).start()

    def backward(step, none):
        chunk = 2 * chunks - 1 - step
        start = chunk * CHUNK

        loads_of(chunk, 3, 4)[0].wait()
        high = high_ref[chunk]
        hh = hh_buf[...]
        dz = jnp.dot(high, hh, preferred_element_type=jnp.float32)
        dz += jnp.dot(low_ref[chunk], hh, preferred_element_type=jnp.float32)
        dz += jnp.dot(high, hl_buf[...], preferred_element_type=jnp.float32)
        dz_ref[...] = dz.reshape(dz_ref.shape)
        right = carry_ref[...]
        upper = fx_ref[start + CHUNK + 1]
        here = fx_ref[start + CHUNK]
        for i in range(CHUNK - 1, -1, -1):
            lower = fx_ref[start + i]
            rate = SUM_COEF * (right - left_ref[start + i]) + DIFF_COEF * (upper - lower)
            part_ref[:, start + i] = rate + dz_ref[:, i] - (5.0 / 9.0) * reg_buf[:, start + i]
            right = here + ROOT * right
            upper = here
            here = lower
        carry_ref[...] = right
        return none

    enter()
    zw_load.wait()
    lax.fori_loop(0, chunks, forward, jnp.float32(1.0), unroll=True)
    send()
    for copy in table_loads():
        copy.wait()
    lax.fori_loop(chunks, 2 * chunks, backward, 0, unroll=True)
    for n in range(4):
        copy_of(n).wait()
    xr_out[...] = xr_got[...]
    xl_out[...] = xl_got[...]
    zr_out[...] = zr_got[...]
    zl_out[...] = zl_got[...]


def final_kernel(
    part_ref, cell_ref, xr_ref, xl_ref, zr_ref, zl_ref, cz_ref,
    state_out, out_out, state_ref, out_ref, stack_ref, dz_ref, store_sem,
):
    chunks = zr_ref.shape[0]
    stores = []
    for c in range(chunks):
        at = pl.ds(c * CHUNK, CHUNK)
        ends = ((out_ref.at[:, at], out_out.at[:, at]), (state_ref.at[:, at], state_out.at[:, at]))
        stores.append([
            pltpu.make_async_copy(source, target, store_sem.at[c, n])
            for n, (source, target) in enumerate(ends)
        ])
    stack_ref[12:16] = jnp.zeros((4, stack_ref.shape[1]), jnp.float32)
    for c in range(chunks):
        zr = zr_ref[c]
        zl = zl_ref[c]
        zr_high = zr.astype(jnp.bfloat16).astype(jnp.float32)
        zl_high = zl.astype(jnp.bfloat16).astype(jnp.float32)
        stack_ref[0:2] = zr_high
        stack_ref[2:4] = zl_high
        stack_ref[4:6] = zr - zr_high
        stack_ref[6:8] = zl - zl_high
        stack_ref[8:10] = zr_high
        stack_ref[10:12] = zl_high
        dz = lax.dot_general(
            stack_ref[...].astype(jnp.bfloat16), cz_ref[...], (((0,), (0,)), ((), ())),
            preferred_element_type=jnp.float32,
        )
        dz_ref[...] = dz.reshape(dz_ref.shape)
        left = (-SUM_COEF * ROOT ** (c * CHUNK)) * xr_ref[0]
        right = (SUM_COEF * ROOT ** ((chunks - 1 - c) * CHUNK)) * xl_ref[0]
        for i in range(CHUNK):
            row = c * CHUNK + i
            fresh = part_ref[:, row] + dz_ref[:, i]
            fresh += ROOT**i * left + ROOT ** (CHUNK - 1 - i) * right
            if row == 0:
                fresh -= DIFF_COEF * xr_ref[1]
            if row == chunks * CHUNK - 1:
                fresh += DIFF_COEF * xl_ref[1]
            out_ref[:, row] = fresh
            state_ref[:, row] = cell_ref[:, row] + (15.0 / 16.0) * fresh
        for copy in stores[c]:
            copy.start()
    for copy in sum(stores, []):
        copy.wait()


def per_device(density, momentum, energy, register):
    nx, ny, nz = density.shape
    chunks = nx // CHUNK
    rows = CHUNK * ny
    f32, bf16 = jnp.float32, jnp.bfloat16
    vmem = pl.BlockSpec(memory_space=pltpu.VMEM)
    hbm = pl.BlockSpec(memory_space=pl.ANY)
    far = lambda value: pltpu.with_memory_space_constraint(value, pltpu.HBM)
    close = lambda value: pltpu.with_memory_space_constraint(value, pltpu.VMEM)
    edge_x = (2, 5, ny, nz)
    edge_z = (chunks, 2, 5 * rows)
    full = (5, nx, ny, nz)
    buffers = [pltpu.VMEM(edge_x, f32)] * 2 + [pltpu.VMEM(edge_z, f32)] * 2
    high, low = local_table(nz)

    kept = pl.pallas_call(
        local_kernel,
        in_specs=[hbm] * 8,
        out_specs=[vmem] * 7,
        out_shape=[
            pltpu.VMEM(shape, f32) for shape in (full, full, edge_x, edge_x, edge_z, edge_z)
        ]
        + [pltpu.VMEM((16, nz), bf16)],
        scratch_shapes=buffers * 2
        + [
            pltpu.VMEM((nx + 2, 5, ny, nz), f32),
            pltpu.VMEM((nx, 5, ny, nz), f32),
            pltpu.VMEM((chunks, 5 * rows, nz), bf16),
            pltpu.VMEM((chunks, 5 * rows, nz), bf16),
            pltpu.VMEM((5, CHUNK, ny, nz), f32),
            pltpu.VMEM((5, ny, nz), f32),
            pltpu.VMEM(full, f32),
            pltpu.VMEM((nz, nz), bf16),
            pltpu.VMEM((nz, nz), bf16),
            pltpu.VMEM((16, nz), bf16),
            pltpu.SemaphoreType.DMA((4,)),
            pltpu.SemaphoreType.DMA((4,)),
            pltpu.SemaphoreType.DMA((chunks, 4)),
            pltpu.SemaphoreType.DMA((4,)),
        ],
        compiler_params=pltpu.CompilerParams(
            vmem_limit_bytes=36 * 1024 * 1024, collective_id=0, has_side_effects=True
        ),
        name="local_part",
    )(
        far(density), far(momentum), far(energy), far(register),
        far(jnp.asarray(summary_table(nz))), far(jnp.asarray(high)), far(jnp.asarray(low)),
        far(jnp.asarray(correction_table(nz))),
    )

    return pl.pallas_call(
        final_kernel,
        in_specs=[vmem] * 7,
        out_specs=[hbm, hbm],
        out_shape=[jax.ShapeDtypeStruct(full, f32)] * 2,
        scratch_shapes=[pltpu.VMEM(full, f32)] * 2
        + [
            pltpu.VMEM((16, 5 * rows), f32),
            pltpu.VMEM((5, CHUNK, ny, nz), f32),
            pltpu.SemaphoreType.DMA((chunks, 2)),
        ],
        compiler_params=pltpu.CompilerParams(vmem_limit_bytes=36 * 1024 * 1024),
        name="neighbour_part",
    )(*(close(value) for value in kept))


def solution(mesh):
    specs = (
        P("gx", None, "gz"),
        P(None, "gx", None, "gz"),
        P("gx", None, "gz"),
        P(None, "gx", None, "gz"),
    )
    out = P(None, "gx", None, "gz")
    return jax.shard_map(
        per_device, mesh=mesh, in_specs=specs, out_specs=(out, out), check_vma=False
    )
```
